256 devices in a mesh: row: 8 (over z_hi, x), col: 32 (over z_lo, y, core).
Axes of the slice: x: 4, y: 4, z: 8 (z_hi: 2, z_lo: 4; z = z_hi * 4 + z_lo), core: 2. Of those that a mesh axis runs over, the one named last changes fastest.
Arguments:
- amplitudes: bfloat16 [32768, 4096], P('col', 'row'), may hold values from -6 to 6
- amplitude_mask: int32 [256, 32], P('col', 'row'), may hold values 0 or 1
- integrals: bfloat16 [4096, 8192], P('col', 'row'), may hold values from -0.09375 to 0.09375
- integral_mask: int32 [32, 64], P('col', 'row'), may hold values 0 or 1
- residual_in: bfloat16 [32768, 8192], P('col', 'row'), may hold values from -6 to 6
- residual_mask: int32 [256, 64], P('col', 'row'), may hold values 0 or 1
Outputs:
- residual_out: float32 [32768, 8192], P('col', 'row')
The draws below stay inside these ranges and needn't reach their ends.
All inputs are finite; a program needn't handle non-finite values. No bound on the sum of `amplitude_mask` or of `integral_mask` or of `residual_mask` on one device may be relied on, other than what follows from the above.
Results may differ from the reference program's by a relative error of at most 0.0003.
Values may be sent and summed in bfloat16 or wider, within the bound.
A program may use at most 64 MiB of HBM per device.

```python
import jax
import jax.numpy as jnp

TILE = 128
MT = 256
NT = 64
KT = 32


def set_ends(drawn, own_key, low, largest):
    place = [jax.random.randint(jax.random.fold_in(own_key, axis), (), 0, length) for axis, length in enumerate(drawn.shape)]
    main_axis = drawn.shape.index(max(drawn.shape))
    next_to = place[:main_axis] + [(place[main_axis] + 1) % drawn.shape[main_axis]] + place[main_axis + 1:]
    return drawn.at[tuple(place)].set(low).at[tuple(next_to)].set(largest)


def levels(own_key, dims, cuts, smallest, high):
    gain = 1.0
    for position, shards_of in cuts:
        draws = jax.random.uniform(jax.random.fold_in(jax.random.fold_in(own_key, 6), position), (shards_of,), jnp.float32, smallest / len(cuts), high / len(cuts))
        gain = gain * jnp.repeat(jnp.exp(draws), dims[position] // shards_of).reshape((-1,) + (1,) * (len(dims) - 1 - position))
    return gain


def normal_values(key, extent, width, limit, cuts=(), held_as=jnp.bfloat16):
    result = jax.random.normal(key, extent, jnp.float32) * width
    if len(cuts) > 0:
        result = levels(key, extent, cuts, -0.22, 0.18) * result
    return jnp.clip(result, min=-limit, max=limit).astype(held_as)


def setup_inputs(seed: int = 0) -> dict:
    key_list = jax.random.split(jax.random.key(seed), 7)
    return {
        "amplitudes": normal_values(key_list[0], (MT * TILE, KT * TILE), 1.0, 6.0, ((0, 32), (1, 8))),
        "amplitude_mask": set_ends((jax.random.randint(key_list[1], (MT, KT), 0, 4) < 3).astype(jnp.int32), jax.random.fold_in(key_list[1], 1), 0, 1),
        "integrals": normal_values(key_list[2], (KT * TILE, NT * TILE), (KT * TILE) ** -0.5, 0.09375, ((0, 32), (1, 8))),
        "integral_mask": set_ends((jax.random.randint(key_list[3], (KT, NT), 0, 4) < 3).astype(jnp.int32), jax.random.fold_in(key_list[3], 1), 0, 1),
        "residual_in": normal_values(key_list[4], (MT * TILE, NT * TILE), 1.0, 6.0, ((0, 32), (1, 8))),
        "residual_mask": set_ends((jax.random.randint(key_list[5], (MT, NT), 0, 4) < 3).astype(jnp.int32), jax.random.fold_in(key_list[5], 1), 0, 1),
    }


def screen(values, tile_mask):
    above, across = tile_mask.shape
    blocks = values.reshape(above, TILE, across, TILE)
    factor = tile_mask.astype(values.dtype)[:, None, :, None]
    return (blocks * factor).reshape(values.shape)


def reference(amplitudes, amplitude_mask, integrals, integral_mask, residual_in, residual_mask):
    screened_amplitudes = screen(amplitudes, amplitude_mask)
    screened_integrals = screen(integrals, integral_mask)
    ladder = jnp.dot(screened_amplitudes, screened_integrals, preferred_element_type=jnp.float32)
    return residual_in.astype(jnp.float32) + screen(ladder, residual_mask)
```

```python
import functools

import jax
import jax.numpy as jnp
from jax import lax
from jax.experimental import pallas as pl
from jax.experimental.pallas import tpu as pltpu
from jax.sharding import PartitionSpec as P

MESH = pl.DeviceIdType.MESH
TILE = 128
XROWS = (128, 128, 128, 128)
ZROWS = (64, 64, 64, 64, 64, 64, 64, 64)
FIRST = 2
ZNEXT = 2
LAG = 2

ORDER = [
    ("xo", 1, 1, 0), ("xo", -1, -1, 0), ("xo", 1, 1, 1), ("xo", -1, -1, 1), ("vz", 1, 1), ("vz", -1, 1), ("vy", 1, 0),
    ("vy", -1, 0), ("z", 1, 1, 0), ("z", -1, 1, 0), ("xo", 1, 1, 2), ("xo", -1, -1, 2), ("z", 1, 1, 1),
    ("z", -1, 1, 1), ("xo", 1, 1, 3), ("xo", -1, -1, 3), ("vy", 1, -1), ("vy", -1, -1), ("vz", 1, 2), ("vz", -1, 2),
    ("z", 1, 2, 0), ("z", -1, 2, 0), ("z", 1, 2, 1), ("z", -1, 2, 1), ("vy", 1, 1), ("vy", -1, 1), ("vyf", 1, 0),
    ("vyf", -1, 0), ("vz", 1, 3), ("vz", -1, 3), ("z", 1, 3, 0), ("z", -1, 3, 0), ("vyf", 1, -1), ("vyf", -1, -1),
    ("z", 1, 1, 2), ("z", -1, 1, 2), ("z", 1, 3, 1), ("z", -1, 3, 1), ("z", 1, 1, 3), ("z", -1, 1, 3), ("vy", -1, -2),
    ("vy", 1, 2), ("vy", 1, -2), ("vy", -1, 2), ("z", 1, 4, 0), ("z", -1, 4, 0), ("vy", 1, -3), ("vy", -1, -3),
    ("vy", 1, 3), ("vy", -1, 3), ("z", 1, 2, 2), ("z", -1, 2, 2), ("vyf", 1, 1), ("vyf", -1, 1), ("z", -1, 4, 1),
    ("z", 1, 4, 1), ("z", -1, 2, 3), ("z", 1, 2, 3), ("po", 1, 1, 0), ("vyf", 1, 2), ("vyf", 1, -2), ("vyf", -1, 2),
    ("vyf", -1, -2), ("z", 1, 3, 2), ("z", -1, 3, 2), ("vyf", 1, 3), ("vyf", -1, -3), ("po", -1, -1, 0),
    ("vyf", 1, -3), ("vyf", -1, 3), ("z", 1, 1, 4), ("z", -1, 1, 4), ("po", -1, -1, 1), ("vk", 0, 0, 0),
    ("vk", 0, 0, -1), ("vk", 0, 0, 1), ("vk", 1, 1, 0), ("vk", 1, -1, 0), ("xo", 1, -1, 0), ("xo", -1, 1, 0),
    ("vk", 1, 1, -1), ("xo", 1, -1, 1), ("vk", 1, -1, -1), ("xo", -1, 1, 1), ("vk", 0, 0, -2), ("vk", 0, 0, 2),
    ("xo", 1, -1, 2), ("xo", -1, 1, 2), ("vk", 1, 1, 1), ("vk", 1, -1, 1), ("xo", 1, -1, 3), ("xo", -1, 1, 3),
    ("vk", 2, 1, 0), ("vk", 2, -1, 0), ("xf", 1, 1, 0), ("xf", -1, -1, 0), ("vk", 0, 0, -3), ("vk", 0, 0, 3),
    ("vk", 2, 1, -1), ("xf", 1, 1, 1), ("xf", -1, -1, 1), ("vk", 2, -1, -1), ("xf", 1, 1, 2), ("xf", -1, -1, 2),
    ("vk", 1, 1, 2), ("vk", 1, -1, -2), ("vk", 1, 1, -3), ("vk", 1, 1, 3), ("vk", 1, -1, 2), ("vk", 1, 1, -2),
    ("vk", 1, -1, -3), ("xf", 1, 1, 3), ("vk", 1, -1, 3), ("xf", -1, -1, 3), ("vk", 2, 1, 1), ("vk", 2, -1, 1),
    ("vk", 2, 1, 2), ("vk", 2, 1, -2), ("vk", 2, -1, 2), ("vk", 2, -1, -2), ("vk", 2, 1, 3), ("vk", 2, 1, -3),
    ("vk", 2, -1, -3), ("vk", 2, -1, 3), ("C", "oc", 0), ("po", 1, 1, 1), ("z", 1, 3, 3), ("z", -1, 3, 3),
    ("po", -1, 1, 0), ("po", -1, 1, 1), ("C", "p3", 0), ("z", 1, 1, 5), ("C", "oc", 1), ("z", -1, 1, 5),
    ("z", 1, 4, 2), ("z", -1, 4, 2), ("C", "oc", 2), ("pf", 1, 1, 0), ("pf", 1, 1, 1), ("C", "pl", 0), ("z", 1, 2, 4),
    ("z", -1, 2, 4), ("C", "oc", 3), ("C", "oc", 4), ("z", 1, 4, 3), ("po", 1, -1, 0), ("po", 1, -1, 1),
    ("C", "p3", 4), ("z", -1, 4, 3), ("pf", -1, -1, 0), ("pf", -1, -1, 1), ("C", "pl", 4), ("C", "oc", 5),
    ("z", 1, 2, 5), ("z", -1, 2, 5), ("C", "oc", 6), ("po", 1, 1, 2), ("po", -1, -1, 2), ("C", "oc", 7),
    ("z", 1, 3, 4), ("z", -1, 3, 4), ("z", 1, 1, 6), ("z", -1, 1, 6), ("po", 1, 1, 3), ("po", -1, 1, 2),
    ("po", -1, 1, 3), ("C", "p3", 1), ("po", 1, -1, 2), ("po", 1, -1, 3), ("po", -1, -1, 3), ("C", "p3", 5),
    ("z", 1, 3, 5), ("z", -1, 3, 5), ("z", 1, 1, 7), ("z", -1, 1, 7), ("z", 1, 4, 4), ("z", -1, 4, 4),
    ("pf", 1, 1, 2), ("pf", 1, 1, 3), ("C", "pl", 1), ("z", 1, 2, 6), ("z", -1, 2, 6), ("pf", -1, -1, 2),
    ("pf", -1, -1, 3), ("C", "pl", 5), ("z", 1, 4, 5), ("z", -1, 4, 5), ("po", 1, 1, 4), ("z", 1, 2, 7),
    ("z", -1, 2, 7), ("po", -1, -1, 4), ("z", 1, 3, 6), ("z", -1, 3, 6), ("po", 1, 1, 5), ("po", -1, 1, 4),
    ("po", -1, 1, 5), ("C", "p3", 2), ("z", 1, 3, 7), ("z", -1, 3, 7), ("po", 1, -1, 4), ("po", 1, -1, 5),
    ("po", -1, -1, 5), ("C", "p3", 6), ("z", 1, 4, 6), ("z", -1, 4, 6), ("pf", 1, 1, 4), ("pf", 1, 1, 5),
    ("C", "pl", 2), ("z", 1, 4, 7), ("pf", -1, -1, 4), ("pf", -1, -1, 5), ("C", "pl", 6), ("z", -1, 4, 7),
    ("po", 1, 1, 6), ("po", -1, -1, 6), ("po", 1, 1, 7), ("po", -1, 1, 6), ("po", -1, 1, 7), ("C", "p3", 3),
    ("po", 1, -1, 6), ("po", 1, -1, 7), ("po", -1, -1, 7), ("C", "p3", 7), ("pf", -1, -1, 6), ("pf", -1, -1, 7),
    ("C", "pl", 7), ("pf", 1, 1, 6), ("pf", 1, 1, 7), ("C", "pl", 3),
]


def starts():
    out = []
    for same in (1, -1):
        for i in range(len(XROWS)):
            for d in (1, -1):
                out.append((None, ("xo", d, same * d, i)))
    out += [(d, ("vz", d, 1)) for d in (1, -1)]
    out += [(None, ("z", d, 1, j)) for j in range(FIRST) for d in (1, -1)]
    out += [(None, ("vy", d, 0)) for d in (1, -1)]
    out.append((None, ("vk", 0, 0, 0)))
    return out


def follows(event):
    kind, out = event[0], []
    if kind == "xo":
        d, half, i = event[1:]
        if half == d:
            out.append((None, ("xf", d, d, i)))
    if kind == "z":
        d, h, j = event[1:]
        if h < 4:
            out.append((None, ("z", d, h + 1, j)))
        if h == ZNEXT and FIRST <= j + LAG < len(ZROWS):
            out.append((None, ("z", d, 1, j + LAG)))
        if h == 4:
            out += [(None, ("po", 1, d, j)), (None, ("po", -1, d, j))]
    if kind == "po":
        d, half, j = event[1:]
        if half == d:
            out.append((None, ("pf", d, d, j)))
    if kind == "vz":
        d, q = event[1:]
        if q < 3:
            out.append((d, ("vz", d, q + 1)))
        out += [(None, ("vy", 1, -d * q)), (None, ("vy", -1, -d * q))]
        out.append((None, ("vk", 0, 0, -d * q)))
    if kind == "vy":
        d, o = event[1:]
        out += [(None, ("vyf", d, o)), (None, ("vk", 1, d, o))]
    if kind == "vyf":
        d, o = event[1:]
        out.append((None, ("vk", 2, d, o)))
    return out


def offset(event):
    kind = event[0]
    if kind == "vz":
        return -event[1] * event[2]
    if kind in ("vy", "vyf"):
        return event[2]
    return event[3] if kind == "vk" else 0


def rows_of(half, pieces, i):
    return pl.ds((0 if half > 0 else 512) + sum(pieces[:i]), pieces[i])


SEMS = {
    "xo": (2, 2, len(XROWS)),
    "xf": (2, len(XROWS)),
    "z": (2, 4, len(ZROWS)),
    "po": (2, 2, len(ZROWS)),
    "pf": (2, len(ZROWS)),
    "vz": (2, 3),
    "vy": (2, 7),
    "vyf": (2, 7),
    "vk": (3, 2, 7),
}
KINDS = list(SEMS)


def sem_of(event):
    kind = event[0]
    way = lambda d: 0 if d > 0 else 1
    if kind in ("xo", "po"):
        return way(event[1]), way(event[2]), event[3]
    if kind in ("xf", "pf"):
        return way(event[1]), event[3]
    if kind == "z":
        return way(event[1]), event[2] - 1, event[3]
    if kind == "vz":
        return way(event[1]), event[2] - 1
    if kind in ("vy", "vyf"):
        return way(event[1]), event[2] + 3
    return event[1], way(event[2]), event[3] + 3


def kernel(a_in, v_in, res_in, a_mask, v_mask, r_mask, out, a, v, acc, res, relay, load_sem, out_sem, *sems):
    recv = dict(zip(KINDS, sems[: len(KINDS)]))
    sent = dict(zip(KINDS, sems[len(KINDS) :]))
    row, col = lax.axis_index("row"), lax.axis_index("col")
    zh, x = row // 4, row % 4
    zl, y, k = col // 8, (col // 2) % 4, col % 2
    z = 4 * zh + zl

    def at(dx=0, dy=0, dz=0, other=False):
        znew = (z + dz + 8) % 8
        return (
            4 * (znew // 4) + (x + dx + 4) % 4,
            8 * (znew % 4) + 2 * ((y + dy + 4) % 4) + (1 - k if other else k),
        )

    mine = lambda dx: 4 * zh + (x + dx + 4) % 4
    theirs = lambda dx: 4 * (1 - zh) + (x + dx + 4) % 4

    def v_rows(o, dy, half=0):
        start = (8 * (zl + o) + 2 * ((y + dy + 4) % 4) + k) * TILE
        if half == 0:
            return v.at[pl.ds(pl.multiple_of(start, TILE), TILE)]
        start = start + (0 if half > 0 else TILE // 2)
        return v.at[pl.ds(pl.multiple_of(start, TILE // 2), TILE // 2)]

    def copy(event):
        kind = event[0]
        if kind in ("xo", "xf", "po", "pf"):
            d, half, i = event[1:]
            slot = (mine if kind[0] == "x" else theirs)(0 if kind[1] == "o" else -d)
            src = dst = a.at[slot, rows_of(half, XROWS if kind[0] == "x" else ZROWS, i)]
            to = at(dx=d)
        elif kind == "z":
            d, h, j = event[1:]
            rows = rows_of(d, ZROWS, j)
            src = a.at[mine(0), rows] if h == 1 else relay.at[h - 2, rows]
            if h < 4:
                dst = relay.at[h - 1, rows]
            else:
                dst = a.at[4 * (1 - ((z + d + 8) % 8) // 4) + x, rows]
            to = at(dz=d)
        elif kind == "vz":
            d, q = event[1:]
            src = dst = v_rows(-d * (q - 1), 0)
            to = at(dz=d)
        elif kind == "vy":
            d, o = event[1:]
            src = dst = v_rows(o, 0)
            to = at(dy=d)
        elif kind == "vyf":
            d, o = event[1:]
            src = dst = v_rows(o, -d, d)
            to = at(dy=d)
        else:
            via, d, o = event[1:]
            src = dst = v_rows(o, -d * via, d if via == 2 else 0)
            to = at(other=True)
        return pltpu.make_async_remote_copy(
            src_ref=src,
            dst_ref=dst,
            send_sem=sent[kind].at[sem_of(event)],
            recv_sem=recv[kind].at[sem_of(event)],
            device_id=to,
            device_id_type=MESH,
        )

    def within(o, act):
        if o == 0:
            act()
        else:
            pl.when((zl + o >= 0) & (zl + o <= 3))(act)

    copies = []

    def send(step, event):
        copies.append((event, step))
        go = lambda: copy(event).start()
        if step is None:
            go()
        else:
            within(step, go)

    def arrive(event):
        def act():
            copy(event).wait_recv()
            for step, then in follows(event):
                here = lambda then=then: copy(then).start()
                if step is None:
                    here()
                else:
                    within(step, here)

        within(offset(event), act)
        copies.extend((then, (offset(event), step)) for step, then in follows(event))

    def product(slots, rows, cols):
        total = None
        for slot in slots:
            part = jnp.dot(
                a[slot, rows, :],
                v[pl.ds(pl.multiple_of(slot * 512, 512), 512), cols],
                preferred_element_type=jnp.float32,
            )
            total = part if total is None else total + part
        return total

    def multiply(which, c):
        rows = pl.ds(c * TILE, TILE)
        width = 512
        slots = {
            "oc": [mine(dx) for dx in (0, 1, 2, 3)],
            "p3": [theirs(dx) for dx in (0, 1, 3)],
            "pl": [theirs(2)],
        }[which]

        def columns(n, carry):
            cols = pl.ds(pl.multiple_of(n * width, width), width)
            total = product(slots, rows, cols)
            if which == "oc":
                acc[rows, cols] = total
            elif which == "p3":
                acc[rows, cols] += total
            else:
                total = total + acc[rows, cols]
                for t in range(width // TILE):
                    tile = pl.ds(pl.multiple_of(n * width + t * TILE, TILE), TILE)
                    keep = r_mask[c, n * (width // TILE) + t].astype(jnp.float32)
                    acc[rows, tile] = res[rows, tile].astype(jnp.float32) + keep * total[:, t * TILE : (t + 1) * TILE]
            return carry

        lax.fori_loop(0, 1024 // width, columns, 0)
        if which == "pl":
            pltpu.make_async_copy(acc.at[rows], out.at[rows], out_sem.at[c]).start()

    own_a = a.at[mine(0)]
    own_v = v_rows(0, 0)
    loads = [
        pltpu.make_async_copy(a_in, own_a, load_sem.at[0]),
        pltpu.make_async_copy(v_in, own_v, load_sem.at[1]),
        pltpu.make_async_copy(res_in, res, load_sem.at[2]),
    ]
    for load in loads:
        load.start()

    barrier = pltpu.get_barrier_semaphore()
    neighbours = [at(dx=1), at(dx=-1), at(dy=1), at(dy=-1), at(dz=1), at(dz=-1), at(other=True)]
    for neighbour in neighbours:
        pl.semaphore_signal(barrier, inc=1, device_id=neighbour, device_id_type=MESH)

    loads[0].wait()

    def screen_a(i, carry):
        rows = pl.ds(pl.multiple_of(i * TILE, TILE), TILE)
        for j in range(4):
            cols = pl.ds(j * TILE, TILE)
            keep = a_mask[i, j].astype(jnp.float32)
            a[mine(0), rows, cols] = (a[mine(0), rows, cols].astype(jnp.float32) * keep).astype(jnp.bfloat16)
        return carry

    lax.fori_loop(0, 8, screen_a, 0)
    loads[1].wait()
    own_rows = pl.ds(pl.multiple_of(col * TILE, TILE), TILE)
    for j in range(8):
        cols = pl.ds(j * TILE, TILE)
        keep = v_mask[0, j].astype(jnp.float32)
        v[own_rows, cols] = (v[own_rows, cols].astype(jnp.float32) * keep).astype(jnp.bfloat16)
    pl.semaphore_wait(barrier, len(neighbours))

    for step, event in starts():
        go = lambda event=event: copy(event).start()
        if step is None:
            go()
        else:
            within(step, go)
        copies.append((event, (0, step)))

    loads[2].wait()
    for op in ORDER:
        if op[0] == "C":
            multiply(op[1], op[2])
        else:
            arrive(op)

    for event, (o, step) in copies:
        def done(event=event, step=step):
            if step is None:
                copy(event).wait_send()
            else:
                within(step, lambda: copy(event).wait_send())

        within(o, done)
    for c in range(8):
        rows = pl.ds(c * TILE, TILE)
        pltpu.make_async_copy(acc.at[rows], out.at[rows], out_sem.at[c]).wait()


def local(amplitudes, amplitude_mask, integrals, integral_mask, residual_in, residual_mask):
    hbm = pl.BlockSpec(memory_space=pl.ANY)
    smem = pl.BlockSpec(memory_space=pltpu.SMEM)
    semaphores = [pltpu.SemaphoreType.DMA(shape) for shape in SEMS.values()]
    return pl.pallas_call(
        kernel,
        out_shape=jax.ShapeDtypeStruct((1024, 1024), jnp.float32),
        in_specs=[hbm, hbm, hbm, smem, smem, smem],
        out_specs=hbm,
        scratch_shapes=[
            pltpu.VMEM((8, 1024, 512), jnp.bfloat16),
            pltpu.VMEM((4096, 1024), jnp.bfloat16),
            pltpu.VMEM((1024, 1024), jnp.float32),
            pltpu.VMEM((1024, 1024), jnp.bfloat16),
            pltpu.VMEM((3, 1024, 512), jnp.bfloat16),
            pltpu.SemaphoreType.DMA((3,)),
            pltpu.SemaphoreType.DMA((8,)),
            *semaphores,
            *semaphores,
        ],
        compiler_params=pltpu.CompilerParams(
            collective_id=0, has_side_effects=True, vmem_limit_bytes=48 * 1024 * 1024
        ),
        cost_estimate=pl.CostEstimate(flops=2 * 1024 * 4096 * 1024, bytes_accessed=12 << 20, transcendentals=0),
        name="ladder",
    )(amplitudes, integrals, residual_in, amplitude_mask, integral_mask, residual_mask)


def solution(mesh):
    placed = P("col", "row")
    return jax.shard_map(
        local, mesh=mesh, in_specs=(placed,) * 6, out_specs=placed, check_vma=False
    )
```

```python
import functools

import jax
import jax.numpy as jnp
from jax import lax
from jax.experimental import pallas as pl
from jax.experimental.pallas import tpu as pltpu
from jax.sharding import PartitionSpec as P

MESH = pl.DeviceIdType.MESH
TILE = 128
XROWS = (128, 128, 128, 128)
ZROWS = (64, 64, 64, 64, 64, 64, 64, 64)
FIRST = 2
ZNEXT = 2
LAG = 2
ZSTEP = 1
HOPS = 4 // ZSTEP

MROWS = {"oc": 128, "p3": 128, "pl": 128}
NCOLS = {"oc": 512, "p3": 512, "pl": 1024}

ORDER = [
    ("xo", 1, 1, 0), ("xo", -1, -1, 0), ("xo", 1, 1, 1), ("xo", -1, -1, 1), ("vz", 1, 1), ("vz", -1, 1), ("vy", 1, 0),
    ("vy", -1, 0), ("z", 1, 1, 0), ("z", -1, 1, 0), ("xo", 1, 1, 2), ("xo", -1, -1, 2), ("z", 1, 1, 1),
    ("z", -1, 1, 1), ("xo", 1, 1, 3), ("xo", -1, -1, 3), ("vy", 1, -1), ("vy", -1, -1), ("vz", 1, 2), ("vz", -1, 2),
    ("z", 1, 2, 0), ("z", -1, 2, 0), ("z", 1, 2, 1), ("z", -1, 2, 1), ("vy", 1, 1), ("vy", -1, 1), ("vyf", 1, 0),
    ("vyf", -1, 0), ("vz", 1, 3), ("vz", -1, 3), ("z", 1, 3, 0), ("z", -1, 3, 0), ("vyf", 1, -1), ("vyf", -1, -1),
    ("z", 1, 1, 2), ("z", -1, 1, 2), ("z", 1, 3, 1), ("z", -1, 3, 1), ("z", 1, 1, 3), ("z", -1, 1, 3), ("z", 1, 4, 0),
    ("z", -1, 4, 0), ("vy", 1, 2), ("vy", 1, -2), ("vy", 1, -3), ("vy", -1, -2), ("vy", -1, 2), ("vy", -1, -3),
    ("vy", 1, 3), ("vy", -1, 3), ("z", 1, 2, 2), ("z", -1, 2, 2), ("z", 1, 4, 1), ("z", -1, 4, 1), ("vyf", 1, 1),
    ("vyf", -1, 1), ("z", 1, 2, 3), ("z", -1, 2, 3), ("po", 1, 1, 0), ("z", 1, 3, 2), ("z", -1, 3, 2), ("vyf", 1, 2),
    ("vyf", 1, -2), ("vyf", -1, 2), ("vyf", -1, -2), ("po", -1, -1, 0), ("vyf", 1, 3), ("vyf", 1, -3),
    ("vyf", -1, -3), ("z", 1, 1, 4), ("vyf", -1, 3), ("z", -1, 1, 4), ("po", 1, 1, 1), ("z", 1, 3, 3),
    ("z", -1, 3, 3), ("po", -1, -1, 1), ("xo", 1, -1, 0), ("xo", -1, 1, 0), ("xo", 1, -1, 1), ("xo", -1, 1, 1),
    ("xo", 1, -1, 2), ("xo", -1, 1, 2), ("xo", 1, -1, 3), ("xo", -1, 1, 3), ("vk", 0, 0, 0), ("xf", 1, 1, 0),
    ("xf", -1, -1, 0), ("xf", 1, 1, 1), ("xf", -1, -1, 1), ("vk", 0, 0, 1), ("vk", 1, 1, 0), ("vk", 1, -1, 0),
    ("xf", 1, 1, 2), ("xf", -1, -1, 2), ("xf", 1, 1, 3), ("xf", -1, -1, 3), ("vk", 0, 0, 2), ("vk", 1, 1, 1),
    ("vk", 1, -1, 1), ("vk", 2, 1, 0), ("vk", 2, -1, 0), ("vk", 0, 0, 3), ("vk", 1, 1, 2), ("vk", 1, -1, 2),
    ("vk", 1, 1, 3), ("vk", 1, -1, 3), ("vk", 2, 1, 1), ("vk", 2, -1, 1), ("vk", 2, 1, 2), ("vk", 2, -1, 2),
    ("vk", 2, 1, 3), ("vk", 2, -1, 3), ("vk", 0, 0, -1), ("vk", 1, 1, -1), ("vk", 1, -1, -1), ("vk", 2, 1, -1),
    ("vk", 2, -1, -1), ("vk", 0, 0, -2), ("vk", 1, 1, -2), ("vk", 1, -1, -2), ("vk", 2, 1, -2), ("vk", 2, -1, -2),
    ("vk", 0, 0, -3), ("vk", 1, 1, -3), ("vk", 1, -1, -3), ("vk", 2, -1, -3), ("vk", 2, 1, -3), ("C", "oc", 0, 0),
    ("z", 1, 1, 5), ("z", -1, 1, 5), ("C", "oc", 0, 1), ("C", "oc", 1, 0), ("z", 1, 4, 2), ("z", -1, 4, 2),
    ("C", "oc", 1, 1), ("z", 1, 2, 4), ("z", -1, 2, 4), ("C", "oc", 2, 0), ("z", 1, 4, 3), ("C", "oc", 2, 1),
    ("z", -1, 4, 3), ("C", "oc", 3, 0), ("z", 1, 2, 5), ("z", -1, 2, 5), ("po", 1, 1, 2), ("C", "oc", 3, 1),
    ("C", "oc", 4, 0), ("z", 1, 3, 4), ("z", -1, 3, 4), ("po", -1, -1, 2), ("C", "oc", 4, 1), ("z", 1, 1, 6),
    ("z", -1, 1, 6), ("po", 1, 1, 3), ("C", "oc", 5, 0), ("C", "oc", 5, 1), ("z", 1, 3, 5), ("z", -1, 3, 5),
    ("po", -1, -1, 3), ("C", "oc", 6, 0), ("z", 1, 1, 7), ("z", -1, 1, 7), ("C", "oc", 6, 1), ("z", 1, 4, 4),
    ("C", "oc", 7, 0), ("z", -1, 4, 4), ("C", "oc", 7, 1), ("z", 1, 2, 6), ("z", -1, 2, 6), ("po", -1, 1, 0),
    ("po", -1, 1, 1), ("C", "p3", 0, 0), ("C", "p3", 0, 1), ("z", 1, 4, 5), ("z", -1, 4, 5), ("po", 1, 1, 4),
    ("po", 1, -1, 0), ("po", 1, -1, 1), ("C", "p3", 4, 0), ("z", 1, 2, 7), ("C", "p3", 4, 1), ("z", -1, 2, 7),
    ("po", -1, -1, 4), ("po", -1, 1, 2), ("po", -1, 1, 3), ("C", "p3", 1, 0), ("z", 1, 3, 6), ("z", -1, 3, 6),
    ("po", 1, 1, 5), ("C", "p3", 1, 1), ("po", 1, -1, 2), ("po", 1, -1, 3), ("C", "p3", 5, 0), ("po", -1, -1, 5),
    ("z", 1, 3, 7), ("C", "p3", 5, 1), ("z", -1, 3, 7), ("po", -1, 1, 4), ("po", -1, 1, 5), ("C", "p3", 2, 0),
    ("z", 1, 4, 6), ("C", "p3", 2, 1), ("z", -1, 4, 6), ("po", 1, -1, 4), ("po", 1, -1, 5), ("C", "p3", 6, 0),
    ("C", "p3", 6, 1), ("z", 1, 4, 7), ("z", -1, 4, 7), ("pf", 1, 1, 0), ("pf", 1, 1, 1), ("C", "pl", 0, 0),
    ("po", 1, 1, 6), ("pf", -1, -1, 0), ("pf", -1, -1, 1), ("C", "pl", 4, 0), ("pf", 1, 1, 2), ("pf", 1, 1, 3),
    ("C", "pl", 1, 0), ("po", -1, -1, 6), ("pf", -1, -1, 2), ("pf", -1, -1, 3), ("C", "pl", 5, 0), ("pf", 1, 1, 4),
    ("pf", 1, 1, 5), ("C", "pl", 2, 0), ("pf", -1, -1, 4), ("pf", -1, -1, 5), ("C", "pl", 6, 0), ("po", 1, 1, 7),
    ("po", -1, 1, 6), ("po", -1, 1, 7), ("C", "p3", 3, 0), ("po", -1, -1, 7), ("C", "p3", 3, 1), ("po", 1, -1, 6),
    ("po", 1, -1, 7), ("C", "p3", 7, 0), ("C", "p3", 7, 1), ("pf", 1, 1, 6), ("pf", 1, 1, 7), ("C", "pl", 3, 0),
    ("pf", -1, -1, 6), ("pf", -1, -1, 7), ("C", "pl", 7, 0),
]


def starts():
    out = [(d, ("vz", d, 1)) for d in (1, -1)]
    out += [(None, ("z", d, 1, j)) for j in range(FIRST) for d in (1, -1)]
    out += [(None, ("vy", d, 0)) for d in (1, -1)]
    out.append((None, ("vk", 0, 0, 0)))
    return out


def follows(event):
    kind, out = event[0], []
    if kind == "xo":
        d, half, i = event[1:]
        if half == d:
            out.append((None, ("xf", d, d, i)))
    if kind == "z":
        d, h, j = event[1:]
        if h < HOPS:
            out.append((None, ("z", d, h + 1, j)))
        if h == ZNEXT and FIRST <= j + LAG < len(ZROWS):
            out.append((None, ("z", d, 1, j + LAG)))
        if h == HOPS:
            out += [(None, ("po", 1, d, j)), (None, ("po", -1, d, j))]
    if kind == "po":
        d, half, j = event[1:]
        if half == d:
            out.append((None, ("pf", d, d, j)))
    if kind == "vz":
        d, q = event[1:]
        if q < 3:
            out.append((d, ("vz", d, q + 1)))
        out += [(None, ("vy", 1, -d * q)), (None, ("vy", -1, -d * q))]
        out.append((None, ("vk", 0, 0, -d * q)))
    if kind == "vy":
        d, o = event[1:]
        out += [(None, ("vyf", d, o)), (None, ("vk", 1, d, o))]
    if kind == "vyf":
        d, o = event[1:]
        out.append((None, ("vk", 2, d, o)))
    return out


def offset(event):
    kind = event[0]
    if kind == "vz":
        return -event[1] * event[2]
    if kind in ("vy", "vyf"):
        return event[2]
    return event[3] if kind == "vk" else 0


def rows_of(half, pieces, i):
    return pl.ds((0 if half > 0 else 512) + sum(pieces[:i]), pieces[i])


SEMS = {
    "xo": (2, 2, len(XROWS)),
    "xf": (2, len(XROWS)),
    "z": (2, HOPS, len(ZROWS)),
    "po": (2, 2, len(ZROWS)),
    "pf": (2, len(ZROWS)),
    "vz": (2, 3),
    "vy": (2, 7),
    "vyf": (2, 7),
    "vk": (3, 2, 7),
}
KINDS = list(SEMS)


def sem_of(event):
    kind = event[0]
    way = lambda d: 0 if d > 0 else 1
    if kind in ("xo", "po"):
        return way(event[1]), way(event[2]), event[3]
    if kind in ("xf", "pf"):
        return way(event[1]), event[3]
    if kind == "z":
        return way(event[1]), event[2] - 1, event[3]
    if kind == "vz":
        return way(event[1]), event[2] - 1
    if kind in ("vy", "vyf"):
        return way(event[1]), event[2] + 3
    return event[1], way(event[2]), event[3] + 3


def kernel(
    a_in, v_in, res_in, a_mask_in, v_mask_in, r_mask_in, out,
    a, v, res, relay, a_mask, v_mask, r_mask, load_sem, a_sem, *sems
):
    recv = dict(zip(KINDS, sems[: len(KINDS)]))
    sent = dict(zip(KINDS, sems[len(KINDS) :]))
    row, col = lax.axis_index("row"), lax.axis_index("col")
    zh, x = row // 4, row % 4
    zl, y, k = col // 8, (col // 2) % 4, col % 2
    z = 4 * zh + zl

    def at(dx=0, dy=0, dz=0, other=False):
        znew = (z + dz + 8) % 8
        return (
            4 * (znew // 4) + (x + dx + 4) % 4,
            8 * (znew % 4) + 2 * ((y + dy + 4) % 4) + (1 - k if other else k),
        )

    mine = lambda dx: 4 * zh + (x + dx + 4) % 4
    theirs = lambda dx: 4 * (1 - zh) + (x + dx + 4) % 4

    def v_rows(o, dy, half=0):
        start = (8 * (zl + o) + 2 * ((y + dy + 4) % 4) + k) * TILE
        if half == 0:
            return v.at[pl.ds(pl.multiple_of(start, TILE), TILE)]
        start = start + (0 if half > 0 else TILE // 2)
        return v.at[pl.ds(pl.multiple_of(start, TILE // 2), TILE // 2)]

    def copy(event):
        kind = event[0]
        if kind in ("xo", "xf", "po", "pf"):
            d, half, i = event[1:]
            slot = (mine if kind[0] == "x" else theirs)(0 if kind[1] == "o" else -d)
            src = dst = a.at[slot, rows_of(half, XROWS if kind[0] == "x" else ZROWS, i)]
            to = at(dx=d)
        elif kind == "z":
            d, h, j = event[1:]
            rows = rows_of(d, ZROWS, j)
            src = a.at[mine(0), rows] if h == 1 else relay.at[h - 2, rows]
            if h < HOPS:
                dst = relay.at[h - 1, rows]
            else:
                dst = a.at[4 * (1 - ((z + ZSTEP * d + 8) % 8) // 4) + x, rows]
            to = at(dz=ZSTEP * d)
        elif kind == "vz":
            d, q = event[1:]
            src = dst = v_rows(-d * (q - 1), 0)
            to = at(dz=d)
        elif kind == "vy":
            d, o = event[1:]
            src = dst = v_rows(o, 0)
            to = at(dy=d)
        elif kind == "vyf":
            d, o = event[1:]
            src = dst = v_rows(o, -d, d)
            to = at(dy=d)
        else:
            via, d, o = event[1:]
            src = dst = v_rows(o, -d * via, d if via == 2 else 0)
            to = at(other=True)
        return pltpu.make_async_remote_copy(
            src_ref=src,
            dst_ref=dst,
            send_sem=sent[kind].at[sem_of(event)],
            recv_sem=recv[kind].at[sem_of(event)],
            device_id=to,
            device_id_type=MESH,
        )

    def within(o, act):
        if o == 0:
            act()
        else:
            pl.when((zl + o >= 0) & (zl + o <= 3))(act)

    copies = []

    def send(step, event):
        copies.append((event, step))
        go = lambda: copy(event).start()
        if step is None:
            go()
        else:
            within(step, go)

    def arrive(event):
        def act():
            copy(event).wait_recv()
            for step, then in follows(event):
                here = lambda then=then: copy(then).start()
                if step is None:
                    here()
                else:
                    within(step, here)

        within(offset(event), act)
        copies.extend((then, (offset(event), step)) for step, then in follows(event))

    def product(slots, rows, cols):
        total = None
        for slot in slots:
            part = jnp.dot(
                a[slot, rows, :],
                v[pl.ds(pl.multiple_of(slot * 512, 512), 512), cols],
                preferred_element_type=jnp.float32,
            )
            total = part if total is None else total + part
        return total

    def multiply(which, c, n):
        rows = pl.ds(c * MROWS[which], MROWS[which])
        cols = pl.ds(n * NCOLS[which], NCOLS[which])
        slots = {
            "oc": [mine(dx) for dx in (0, 1, 2, 3)],
            "p3": [theirs(dx) for dx in (0, 1, 3)],
            "pl": [theirs(2)],
        }[which]
        total = product(slots, rows, cols)
        if which == "oc":
            out[rows, cols] = total
        elif which == "p3":
            out[rows, cols] += total
        else:
            total = total + out[rows, cols]
            for i in range(MROWS[which] // TILE):
                for j in range(NCOLS[which] // TILE):
                    some = pl.ds(c * MROWS[which] + i * TILE, TILE)
                    tile = pl.ds(n * NCOLS[which] + j * TILE, TILE)
                    keep = r_mask[c * MROWS[which] // TILE + i, n * (NCOLS[which] // TILE) + j].astype(jnp.float32)
                    ladder = keep * total[i * TILE : (i + 1) * TILE, j * TILE : (j + 1) * TILE]
                    out[some, tile] = res[some, tile].astype(jnp.float32) + ladder

    own_a = mine(0)
    own_v = pl.ds(pl.multiple_of(col * TILE, TILE), TILE)
    loads = {
        "am": pltpu.make_async_copy(a_mask_in, a_mask, load_sem.at[0]),
        "vm": pltpu.make_async_copy(v_mask_in, v_mask, load_sem.at[1]),
        "v": pltpu.make_async_copy(v_in, v.at[own_v], load_sem.at[2]),
        "res": pltpu.make_async_copy(res_in, res, load_sem.at[3]),
        "rm": pltpu.make_async_copy(r_mask_in, r_mask, load_sem.at[4]),
    }
    for half in (1, -1):
        for i in range(len(XROWS)):
            rows = rows_of(half, XROWS, i)
            loads[half, i] = pltpu.make_async_copy(
                a_in.at[rows], a.at[own_a, rows], a_sem.at[0 if half > 0 else 1, i]
            )
    for load in loads.values():
        load.start()

    barrier = pltpu.get_barrier_semaphore()
    neighbours = [at(dx=1), at(dx=-1), at(dy=1), at(dy=-1), at(dz=1), at(dz=-1), at(other=True)]
    if ZSTEP > 1:
        neighbours += [at(dz=ZSTEP), at(dz=-ZSTEP)]
    for neighbour in neighbours:
        pl.semaphore_signal(barrier, inc=1, device_id=neighbour, device_id_type=MESH)

    loads["am"].wait()
    loads["vm"].wait()

    def screen_a(half, i):
        loads[half, i].wait()
        first = (0 if half > 0 else 512) + sum(XROWS[:i])
        for t in range(first // TILE, (first + XROWS[i]) // TILE):
            rows = pl.ds(t * TILE, TILE)
            for j in range(4):
                cols = pl.ds(j * TILE, TILE)
                keep = a_mask[j, t].astype(jnp.float32)
                a[own_a, rows, cols] = (a[own_a, rows, cols].astype(jnp.float32) * keep).astype(jnp.bfloat16)

    def screen_v():
        loads["v"].wait()
        for j in range(8):
            cols = pl.ds(j * TILE, TILE)
            keep = v_mask[0, j].astype(jnp.float32)
            v[own_v, cols] = (v[own_v, cols].astype(jnp.float32) * keep).astype(jnp.bfloat16)

    def start(step, event):
        go = lambda: copy(event).start()
        if step is None:
            go()
        else:
            within(step, go)
        copies.append((event, (0, step)))

    for i in range(len(XROWS)):
        for half in (1, -1):
            screen_a(half, i)
            if i == 0 and half == 1:
                pl.semaphore_wait(barrier, len(neighbours))
            start(None, ("xo", half, half, i))
        if i == 0:
            screen_v()
            for step, event in starts():
                start(step, event)
    for i in range(len(XROWS)):
        for d in (1, -1):
            start(None, ("xo", d, -d, i))

    loads["res"].wait()
    loads["rm"].wait()
    for op in ORDER:
        if op[0] == "C":
            multiply(*op[1:])
        else:
            arrive(op)

    for event, (o, step) in copies:
        def done(event=event, step=step):
            if step is None:
                copy(event).wait_send()
            else:
                within(step, lambda: copy(event).wait_send())

        within(o, done)


def write(held, out, sem):
    copies = [
        pltpu.make_async_copy(held.at[rows], out.at[rows], sem.at[i])
        for i, rows in enumerate(pl.ds(i * 256, 256) for i in range(4))
    ]
    for copy in copies:
        copy.start()
    for copy in copies:
        copy.wait()


def local(amplitudes, amplitude_mask, integrals, integral_mask, residual_in, residual_mask):
    hbm = pl.BlockSpec(memory_space=pltpu.HBM)
    vmem = pl.BlockSpec(memory_space=pltpu.VMEM)
    semaphores = [pltpu.SemaphoreType.DMA(shape) for shape in SEMS.values()]
    result = pl.pallas_call(
        kernel,
        out_shape=pltpu.VMEM((1024, 1024), jnp.float32),
        in_specs=[hbm] * 6,
        out_specs=vmem,
        scratch_shapes=[
            pltpu.VMEM((8, 1024, 512), jnp.bfloat16),
            pltpu.VMEM((4096, 1024), jnp.bfloat16),
            pltpu.VMEM((1024, 1024), jnp.bfloat16),
            pltpu.VMEM((HOPS - 1, 1024, 512), jnp.bfloat16),
            pltpu.SMEM((4, 8), jnp.int32),
            pltpu.SMEM((1, 8), jnp.int32),
            pltpu.SMEM((8, 8), jnp.int32),
            pltpu.SemaphoreType.DMA((5,)),
            pltpu.SemaphoreType.DMA((2, len(XROWS))),
            *semaphores,
            *semaphores,
        ],
        compiler_params=pltpu.CompilerParams(
            collective_id=0, has_side_effects=True, vmem_limit_bytes=60 * 1024 * 1024 - 65536
        ),
        cost_estimate=pl.CostEstimate(flops=2 * 1024 * 4096 * 1024, bytes_accessed=12 << 20, transcendentals=0),
        name="ladder",
    )(amplitudes, integrals, residual_in, amplitude_mask.T, integral_mask, residual_mask)
    return pl.pallas_call(
        write,
        out_shape=jax.ShapeDtypeStruct((1024, 1024), jnp.float32),
        in_specs=[vmem],
        out_specs=hbm,
        scratch_shapes=[pltpu.SemaphoreType.DMA((4,))],
        compiler_params=pltpu.CompilerParams(vmem_limit_bytes=16 * 1024 * 1024),
        name="write",
    )(result)


def solution(mesh):
    placed = P("col", "row")
    return jax.shard_map(
        local, mesh=mesh, in_specs=(placed,) * 6, out_specs=placed, check_vma=False
    )
```

```python
import functools

import jax
import jax.numpy as jnp
from jax import lax
from jax.experimental import pallas as pl
from jax.experimental.pallas import tpu as pltpu
from jax.sharding import PartitionSpec as P

MESH = pl.DeviceIdType.MESH
TILE = 128
XROWS = (128, 128, 128, 128)
ZROWS = (64, 64, 64, 64, 64, 64, 64, 64)
FIRST = 2
ZSTEP = 1
HOPS = 4 // ZSTEP

MROWS = {"oc": 128, "p3": 128, "pl": 128}
NCOLS = {"oc": 512, "p3": 512, "pl": 1024}

ORDER = [
    ("S", ("xo", -1, 1, 0)), ("vz", 1, 1), ("S", ("xo", -1, 1, 1)), ("vz", -1, 1), ("z", 1, 1, 0),
    ("S", ("xo", -1, 1, 2)), ("xo", 1, 1, 1), ("xo", 1, 1, 2), ("xo", -1, -1, 2), ("xo", -1, -1, 0), ("z", 1, 1, 1),
    ("vy", 1, 0), ("xo", 1, 1, 3), ("vz", 1, 2), ("z", -1, 1, 1), ("S", ("xo", 1, -1, 3)), ("z", 1, 2, 0),
    ("z", -1, 1, 0), ("xo", -1, -1, 3), ("vz", -1, 2), ("vy", -1, 0), ("z", -1, 2, 0), ("S", ("z", -1, 1, 2)),
    ("S", ("xo", 1, -1, 1)), ("vy", 1, 1), ("S", ("xo", 1, -1, 2)), ("xo", 1, 1, 0), ("S", ("xo", 1, -1, 0)),
    ("S", ("z", 1, 1, 2)), ("S", ("z", 1, 1, 3)), ("xo", -1, -1, 1), ("vz", 1, 3), ("vy", -1, -1), ("z", 1, 2, 1),
    ("z", -1, 2, 1), ("S", ("xo", -1, 1, 3)), ("S", ("z", -1, 1, 3)), ("vy", 1, -1), ("z", 1, 1, 2), ("vz", -1, 3),
    ("z", -1, 1, 2), ("z", 1, 3, 0), ("z", -1, 3, 1), ("vyf", 1, 0), ("vy", -1, 1), ("z", 1, 1, 3), ("z", -1, 1, 3),
    ("S", ("z", 1, 1, 4)), ("z", -1, 3, 0), ("S", ("z", -1, 1, 4)), ("z", 1, 2, 2), ("vy", 1, -3), ("vyf", 1, 1),
    ("vy", 1, 2), ("vy", -1, 2), ("S", ("z", 1, 1, 5)), ("vy", -1, -3), ("z", -1, 2, 2), ("vy", -1, 3),
    ("vy", -1, -2), ("vy", 1, -2), ("vyf", -1, 0), ("G", "xo", 1), ("z", 1, 4, 0), ("G", "xf"), ("z", 1, 3, 1),
    ("z", -1, 4, 0), ("S", ("z", -1, 1, 5)), ("G", "xo", -1), ("vy", 1, 3), ("z", -1, 4, 1), ("z", 1, 2, 3),
    ("z", -1, 2, 3), ("vyf", -1, -3), ("z", -1, 3, 2), ("vyf", 1, 2), ("z", -1, 1, 4), ("vyf", -1, -1),
    ("vyf", -1, 2), ("z", 1, 3, 2), ("vyf", 1, -3), ("z", 1, 4, 1), ("po", 1, 1, 0), ("z", 1, 1, 4), ("vyf", 1, -2),
    ("vyf", -1, -2), ("vyf", 1, 3), ("z", 1, 1, 5), ("vyf", -1, 1), ("po", -1, -1, 0), ("vyf", -1, 3),
    ("z", -1, 3, 3), ("vyf", 1, -1), ("z", -1, 4, 2), ("z", 1, 3, 3), ("z", 1, 4, 2), ("z", -1, 1, 5), ("G", "vk"),
    ("S", ("z", -1, 1, 6)), ("z", 1, 2, 4), ("C", "oc", 2, 1), ("C", "oc", 1, 1), ("C", "oc", 2, 0), ("z", -1, 2, 4),
    ("z", -1, 4, 3), ("S", ("z", 1, 1, 6)), ("C", "oc", 3, 0), ("C", "oc", 0, 1), ("z", 1, 2, 5), ("z", -1, 2, 5),
    ("S", ("z", 1, 1, 7)), ("C", "oc", 1, 0), ("z", 1, 4, 3), ("po", 1, 1, 2), ("C", "oc", 5, 0), ("po", -1, -1, 1),
    ("C", "oc", 6, 0), ("S", ("z", -1, 1, 7)), ("C", "oc", 3, 1), ("z", -1, 3, 4), ("po", 1, 1, 1), ("G", "po", 1, 0),
    ("po", -1, -1, 3), ("G", "po", -1, 0), ("z", 1, 3, 4), ("z", -1, 1, 6), ("C", "oc", 5, 1), ("z", 1, 1, 6),
    ("C", "oc", 7, 0), ("C", "oc", 4, 1), ("po", 1, 1, 3), ("C", "oc", 0, 0), ("z", 1, 1, 7), ("z", -1, 3, 5),
    ("po", -1, -1, 2), ("C", "oc", 6, 1), ("C", "oc", 4, 0), ("z", -1, 1, 7), ("z", 1, 4, 4), ("z", 1, 3, 5),
    ("C", "p3", 4, 1), ("G", "po", -1, 1), ("z", -1, 4, 4), ("z", -1, 2, 6), ("z", 1, 2, 6), ("C", "p3", 4, 0),
    ("z", -1, 4, 5), ("z", 1, 2, 7), ("G", "po", 1, 1), ("z", -1, 2, 7), ("z", 1, 4, 5), ("C", "p3", 0, 0),
    ("C", "p3", 1, 1), ("z", 1, 3, 6), ("C", "p3", 5, 1), ("po", 1, 1, 4), ("z", -1, 3, 6), ("G", "po", 1, 2),
    ("po", -1, -1, 5), ("C", "p3", 0, 1), ("G", "pf", 1, 0), ("po", -1, -1, 4), ("C", "p3", 6, 1), ("z", -1, 3, 7),
    ("po", 1, 1, 5), ("G", "po", -1, 2), ("C", "p3", 5, 0), ("z", 1, 3, 7), ("z", 1, 4, 6), ("z", -1, 4, 6),
    ("C", "p3", 1, 0), ("G", "pf", -1, 0), ("C", "pl", 0, 0), ("G", "pf", -1, 1), ("z", -1, 4, 7), ("G", "pf", -1, 2),
    ("z", 1, 4, 7), ("C", "oc", 7, 1), ("G", "pf", 1, 1), ("C", "pl", 1, 0), ("C", "p3", 6, 0), ("C", "p3", 2, 0),
    ("po", -1, -1, 6), ("C", "pl", 5, 0), ("po", 1, 1, 6), ("po", -1, -1, 7), ("C", "pl", 6, 0), ("po", 1, 1, 7),
    ("C", "p3", 2, 1), ("G", "po", -1, 3), ("G", "po", 1, 3), ("C", "p3", 3, 0), ("C", "pl", 4, 0), ("C", "p3", 3, 1),
    ("C", "p3", 7, 0), ("G", "pf", 1, 2), ("C", "pl", 2, 0), ("C", "p3", 7, 1), ("G", "pf", -1, 3), ("C", "pl", 7, 0),
    ("G", "pf", 1, 3), ("C", "pl", 3, 0),
]


def starts():
    out = [(d, ("vz", d, 1)) for d in (1, -1)]
    out += [(None, ("z", d, 1, j)) for j in range(FIRST) for d in (1, -1)]
    out += [(None, ("vy", d, 0)) for d in (1, -1)]
    out.append((None, ("vk", 0, 0, 0)))
    return out


def follows(event):
    kind, out = event[0], []
    if kind == "xo":
        d, half, i = event[1:]
        if half == d:
            out.append((None, ("xf", d, d, i)))
    if kind == "z":
        d, h, j = event[1:]
        if h < HOPS:
            out.append((None, ("z", d, h + 1, j)))
        if h == HOPS:
            out += [(None, ("po", 1, d, j)), (None, ("po", -1, d, j))]
    if kind == "po":
        d, half, j = event[1:]
        if half == d:
            out.append((None, ("pf", d, d, j)))
    if kind == "vz":
        d, q = event[1:]
        if q < 3:
            out.append((d, ("vz", d, q + 1)))
        out += [(None, ("vy", 1, -d * q)), (None, ("vy", -1, -d * q))]
        out.append((None, ("vk", 0, 0, -d * q)))
    if kind == "vy":
        d, o = event[1:]
        out += [(None, ("vyf", d, o)), (None, ("vk", 1, d, o))]
    if kind == "vyf":
        d, o = event[1:]
        out.append((None, ("vk", 2, d, o)))
    return out


def offset(event):
    kind = event[0]
    if kind == "vz":
        return -event[1] * event[2]
    if kind in ("vy", "vyf"):
        return event[2]
    return event[3] if kind == "vk" else 0


def rows_of(half, pieces, i):
    return pl.ds((0 if half > 0 else 512) + sum(pieces[:i]), pieces[i])


def way(d):
    return 0 if d > 0 else 1


def group_of(event):
    kind = event[0]
    if kind == "xo" and event[1] != event[2]:
        return ("xo", event[1])
    if kind in ("xf", "vk"):
        return (kind,)
    if kind == "pf" or kind == "po" and event[1] != event[2]:
        return (kind, event[1], sum(ZROWS[: event[3]]) // TILE)
    return None


RECV = {
    "xo": (2, len(XROWS)),
    "z": (2, HOPS, len(ZROWS)),
    "po": (2, len(ZROWS)),
    "vz": (4,),
    "vy": (2, 4),
    "vyf": (2, 4),
    "Gxo": (2,),
    "Gxf": (1,),
    "Gvk": (1,),
    "Gpo": (2, 4),
    "Gpf": (2, 4),
}
SENT = {"x": (2,), "z": (2,), "y": (2,), "vk": (1,), "vz": (2, 3)}


def kernel(
    a_in, v_in, res_in, a_mask_in, v_mask_in, r_mask_in, out,
    a, v, res, relay, a_mask, v_mask, r_mask, load_sem, a_sem, *sems
):
    recv = dict(zip(RECV, sems[: len(RECV)]))
    sent = dict(zip(SENT, sems[len(RECV) :]))
    row, col = lax.axis_index("row"), lax.axis_index("col")
    zh, x = row // 4, row % 4
    zl, y, k = col // 8, (col // 2) % 4, col % 2
    z = 4 * zh + zl

    def at(dx=0, dy=0, dz=0, other=False):
        znew = (z + dz + 8) % 8
        return (
            4 * (znew // 4) + (x + dx + 4) % 4,
            8 * (znew % 4) + 2 * ((y + dy + 4) % 4) + (1 - k if other else k),
        )

    mine = lambda dx: 4 * zh + (x + dx + 4) % 4
    theirs = lambda dx: 4 * (1 - zh) + (x + dx + 4) % 4

    def v_rows(o, dy, half=0):
        start = (8 * (zl + o) + 2 * ((y + dy + 4) % 4) + k) * TILE
        if half == 0:
            return v.at[pl.ds(pl.multiple_of(start, TILE), TILE)]
        start = start + (0 if half > 0 else TILE // 2)
        return v.at[pl.ds(pl.multiple_of(start, TILE // 2), TILE // 2)]

    def copy(event, sending=True):
        kind = event[0]
        if kind in ("xo", "xf", "po", "pf"):
            d, half, i = event[1:]
            slot = (mine if kind[0] == "x" else theirs)(0 if kind[1] == "o" else -d)
            src = dst = a.at[slot, rows_of(half, XROWS if kind[0] == "x" else ZROWS, i)]
            to = at(dx=d)
        elif kind == "z":
            d, h, j = event[1:]
            rows = rows_of(d, ZROWS, j)
            src = a.at[mine(0), rows] if h == 1 else relay.at[max(h - 2, 0), rows]
            if h < HOPS:
                dst = relay.at[h - 1, rows]
            else:
                dst = a.at[4 * (1 - ((z + ZSTEP * d + 8) % 8) // 4) + x, rows]
            to = at(dz=ZSTEP * d)
        elif kind == "vz":
            d, q = event[1:]
            src = dst = v_rows(-d * (q - 1), 0)
            to = at(dz=d)
        elif kind == "vy":
            d, o = event[1:]
            src = dst = v_rows(o, 0)
            to = at(dy=d)
        elif kind == "vyf":
            d, o = event[1:]
            src = dst = v_rows(o, -d, d)
            to = at(dy=d)
        else:
            via, d, o = event[1:]
            src = dst = v_rows(o, -d * via, d if via == 2 else 0)
            to = at(other=True)
        arrived = recv_sem(event)
        if kind == "vz":
            arrived = arrived[0 if sending else 1]
        return remote(src, dst, sent_sem(event), arrived, to)

    def remote(src, dst, send_sem, recv_sem, to):
        return pltpu.make_async_remote_copy(
            src_ref=src, dst_ref=dst, send_sem=send_sem, recv_sem=recv_sem, device_id=to, device_id_type=MESH
        )

    def sent_sem(event):
        kind = event[0]
        if kind == "vk":
            return sent["vk"].at[0]
        if kind == "vz":
            return sent["vz"].at[way(event[1]), event[2] - 1]
        return sent["z" if kind == "z" else "y" if kind[0] == "v" else "x"].at[way(event[1])]

    def recv_sem(event):
        kind, group = event[0], group_of(event)
        if group is not None:
            return recv["G" + kind].at[tuple([way(group[1]), *group[2:]] if len(group) > 1 else [0])]
        if kind in ("xo", "po"):
            return recv[kind].at[way(event[1]), event[3]]
        if kind == "z":
            return recv[kind].at[way(event[1]), event[2] - 1, event[3]]
        if kind == "vz":
            return recv[kind].at[zl - event[1] * (event[2] - 1)], recv[kind].at[zl - event[1] * event[2]]
        return recv[kind].at[way(event[1]), zl + event[2]]

    def within(o, act):
        if o == 0:
            act()
        else:
            pl.when((zl + o >= 0) & (zl + o <= 3))(act)

    def start(step, event):
        go = lambda: copy(event).start()
        if step is None:
            go()
        else:
            within(step, go)

    def arrive(event):
        def act():
            copy(event, sending=False).wait_recv()
            for step, then in follows(event):
                start(step, then)

        within(offset(event), act)

    def arrive_group(kind, d=1, c=0):
        if kind == "xo":
            rows, slot = pl.ds(0 if d < 0 else 512, 512), mine(-d)
        elif kind == "xf":
            rows, slot = pl.ds(0, 1024), mine(2)
        elif kind == "po":
            rows, slot = pl.ds((0 if d < 0 else 512) + c * TILE, TILE), theirs(-d)
        elif kind == "pf":
            rows, slot = pl.ds((0 if d > 0 else 512) + c * TILE, TILE), theirs(2)
        held = v.at[pl.ds(0, 2048)] if kind == "vk" else a.at[slot, rows]
        sem = recv["G" + kind].at[tuple([way(d), c][: len(RECV["G" + kind])])]
        remote(held, held, sent["vk"].at[0], sem, at(other=True)).wait_recv()

    def departures():
        for d in (1, -1):
            for kind, held in (("x", a.at[pl.ds(0, 3)]), ("z", a.at[pl.ds(0, HOPS), pl.ds(0, 512)]), ("y", v.at[pl.ds(0, 768)])):
                remote(held, held, sent[kind].at[way(d)], recv["Gvk"].at[0], at(other=True)).wait_send()
            for q in (1, 2, 3):
                leave = lambda: copy(("vz", d, q)).wait_send()
                within(d, lambda: within(-d * (q - 1), leave))
        held = v.at[pl.ds(0, 2048)]
        remote(held, held, sent["vk"].at[0], recv["Gvk"].at[0], at(other=True)).wait_send()

    def product(slots, rows, cols):
        total = None
        for slot in slots:
            part = jnp.dot(
                a[slot, rows, :],
                v[pl.ds(pl.multiple_of(slot * 512, 512), 512), cols],
                preferred_element_type=jnp.float32,
            )
            total = part if total is None else total + part
        return total

    def multiply(which, c, n):
        rows = pl.ds(c * MROWS[which], MROWS[which])
        cols = pl.ds(n * NCOLS[which], NCOLS[which])
        slots = {
            "oc": [mine(dx) for dx in (0, 1, 2, 3)],
            "p3": [theirs(dx) for dx in (0, 1, 3)],
            "pl": [theirs(2)],
        }[which]
        total = product(slots, rows, cols)
        if which == "oc":
            out[rows, cols] = total
        elif which == "p3":
            out[rows, cols] += total
        else:
            total = total + out[rows, cols]
            for i in range(MROWS[which] // TILE):
                for j in range(NCOLS[which] // TILE):
                    some = pl.ds(c * MROWS[which] + i * TILE, TILE)
                    tile = pl.ds(n * NCOLS[which] + j * TILE, TILE)
                    keep = r_mask[c * MROWS[which] // TILE + i, n * (NCOLS[which] // TILE) + j].astype(jnp.float32)
                    ladder = keep * total[i * TILE : (i + 1) * TILE, j * TILE : (j + 1) * TILE]
                    out[some, tile] = res[some, tile].astype(jnp.float32) + ladder

    own_a = mine(0)
    own_v = pl.ds(pl.multiple_of(col * TILE, TILE), TILE)
    loads = {
        "am": pltpu.make_async_copy(a_mask_in, a_mask, load_sem.at[0]),
        "vm": pltpu.make_async_copy(v_mask_in, v_mask, load_sem.at[1]),
        "v": pltpu.make_async_copy(v_in, v.at[own_v], load_sem.at[2]),
        "res": pltpu.make_async_copy(res_in, res, load_sem.at[3]),
        "rm": pltpu.make_async_copy(r_mask_in, r_mask, load_sem.at[4]),
    }
    for half in (1, -1):
        for i in range(len(XROWS)):
            rows = rows_of(half, XROWS, i)
            loads[half, i] = pltpu.make_async_copy(
                a_in.at[rows], a.at[own_a, rows], a_sem.at[0 if half > 0 else 1, i]
            )
    for load in loads.values():
        load.start()

    barrier = pltpu.get_barrier_semaphore()
    neighbours = [at(dx=1), at(dx=-1), at(dy=1), at(dy=-1), at(dz=1), at(dz=-1), at(other=True)]
    if ZSTEP > 1:
        neighbours += [at(dz=ZSTEP), at(dz=-ZSTEP)]
    for neighbour in neighbours:
        pl.semaphore_signal(barrier, inc=1, device_id=neighbour, device_id_type=MESH)

    loads["am"].wait()
    loads["vm"].wait()

    def screen_a(half, i):
        loads[half, i].wait()
        first = (0 if half > 0 else 512) + sum(XROWS[:i])
        for t in range(first // TILE, (first + XROWS[i]) // TILE):
            rows = pl.ds(t * TILE, TILE)
            for j in range(4):
                cols = pl.ds(j * TILE, TILE)
                keep = a_mask[j, t].astype(jnp.float32)
                a[own_a, rows, cols] = (a[own_a, rows, cols].astype(jnp.float32) * keep).astype(jnp.bfloat16)

    def screen_v():
        loads["v"].wait()
        for j in range(8):
            cols = pl.ds(j * TILE, TILE)
            keep = v_mask[0, j].astype(jnp.float32)
            v[own_v, cols] = (v[own_v, cols].astype(jnp.float32) * keep).astype(jnp.bfloat16)

    for i in range(len(XROWS)):
        for half in (1, -1):
            screen_a(half, i)
            if i == 0 and half == 1:
                pl.semaphore_wait(barrier, len(neighbours))
            start(None, ("xo", half, half, i))
        if i == 0:
            screen_v()
            for step, event in starts():
                start(step, event)
    loads["res"].wait()
    loads["rm"].wait()
    for op in ORDER:
        if op[0] == "C":
            multiply(*op[1:])
        elif op[0] == "G":
            arrive_group(*op[1:])
        elif op[0] == "S":
            start(None, op[1])
        else:
            arrive(op)
    departures()


def write(held, out, sem):
    copies = [
        pltpu.make_async_copy(held.at[rows], out.at[rows], sem.at[i])
        for i, rows in enumerate(pl.ds(i * 256, 256) for i in range(4))
    ]
    for copy in copies:
        copy.start()
    for copy in copies:
        copy.wait()


def local(amplitudes, amplitude_mask, integrals, integral_mask, residual_in, residual_mask):
    hbm = pl.BlockSpec(memory_space=pltpu.HBM)
    vmem = pl.BlockSpec(memory_space=pltpu.VMEM)
    semaphores = [pltpu.SemaphoreType.DMA(shape) for shape in [*RECV.values(), *SENT.values()]]
    result = pl.pallas_call(
        kernel,
        out_shape=pltpu.VMEM((1024, 1024), jnp.float32),
        in_specs=[hbm] * 6,
        out_specs=vmem,
        scratch_shapes=[
            pltpu.VMEM((8, 1024, 512), jnp.bfloat16),
            pltpu.VMEM((4096, 1024), jnp.bfloat16),
            pltpu.VMEM((1024, 1024), jnp.bfloat16),
            pltpu.VMEM((max(HOPS - 1, 1), 1024, 512), jnp.bfloat16),
            pltpu.SMEM((4, 8), jnp.int32),
            pltpu.SMEM((1, 8), jnp.int32),
            pltpu.SMEM((8, 8), jnp.int32),
            pltpu.SemaphoreType.DMA((5,)),
            pltpu.SemaphoreType.DMA((2, len(XROWS))),
            *semaphores,
        ],
        compiler_params=pltpu.CompilerParams(
            collective_id=0, has_side_effects=True, vmem_limit_bytes=60 * 1024 * 1024 - 65536
        ),
        cost_estimate=pl.CostEstimate(flops=2 * 1024 * 4096 * 1024, bytes_accessed=12 << 20, transcendentals=0),
        name="ladder",
    )(amplitudes, integrals, residual_in, amplitude_mask.T, integral_mask, residual_mask)
    return pl.pallas_call(
        write,
        out_shape=jax.ShapeDtypeStruct((1024, 1024), jnp.float32),
        in_specs=[vmem],
        out_specs=hbm,
        scratch_shapes=[pltpu.SemaphoreType.DMA((4,))],
        compiler_params=pltpu.CompilerParams(vmem_limit_bytes=16 * 1024 * 1024),
        name="write",
    )(result)


def solution(mesh):
    placed = P("col", "row")
    return jax.shard_map(
        local, mesh=mesh, in_specs=(placed,) * 6, out_specs=placed, check_vma=False
    )
```

```python
import functools

import jax
import jax.numpy as jnp
from jax import lax
from jax.experimental import pallas as pl
from jax.experimental.pallas import tpu as pltpu
from jax.sharding import PartitionSpec as P

MESH = pl.DeviceIdType.MESH
TILE = 128
XROWS = (128, 128, 128, 128)
ZROWS = (64, 64, 64, 64, 64, 64, 64, 64)
FIRST = 1
ZSTEP = 1
HOPS = 4 // ZSTEP

MROWS = {"oc": 128, "p3": 128, "pl": 128}
NCOLS = {"oc": 512, "p3": 512, "pl": 1024}
LAST = (3, 7)

ORDER = [
    ("S", ("z", 1, 1, 1), 0), ("S", ("xo", -1, 1, 2)), ("S", ("z", -1, 1, 1), 2), ("S", ("z", -1, 1, 1), 1),
    ("S", ("z", 1, 1, 1), 3), ("S", ("xo", 1, -1, 0)), ("S", ("z", 1, 1, 1), 2), ("S", ("z", 1, 1, 2), 0),
    ("vz", 1, 1), ("S", ("z", 1, 1, 1), 1), ("S", ("z", -1, 1, 1), 0), ("vz", -1, 1), ("z", 1, 1, 0), ("xo", 1, 1, 1),
    ("S", ("z", -1, 1, 2), 1), ("S", ("z", -1, 1, 3), 1), ("xo", 1, 1, 2), ("S", ("z", 1, 1, 2), 3),
    ("S", ("xo", 1, -1, 2)), ("S", ("z", 1, 1, 3), 0), ("S", ("z", 1, 1, 2), 1), ("S", ("xo", -1, 1, 3)),
    ("z", -1, 1, 1), ("S", ("xo", 1, -1, 1)), ("S", ("xo", -1, 1, 0)), ("S", ("z", -1, 1, 1), 3), ("z", -1, 1, 0),
    ("vz", 1, 2), ("S", ("z", 1, 1, 4), 0), ("z", 1, 2, 0), ("vz", -1, 2), ("xo", -1, -1, 3),
    ("S", ("z", 1, 1, 3), 3), ("z", -1, 2, 1), ("vy", -1, -1), ("S", ("z", 1, 1, 4), 3), ("vy", 1, 0),
    ("xo", 1, 1, 0), ("S", ("z", -1, 1, 2), 2), ("z", 1, 1, 1), ("S", ("z", 1, 1, 2), 2), ("S", ("z", -1, 1, 3), 2),
    ("S", ("z", -1, 1, 2), 0), ("S", ("z", -1, 1, 2), 3), ("vy", 1, 1), ("S", ("z", 1, 1, 3), 1),
    ("S", ("xo", -1, 1, 1)), ("S", ("z", -1, 1, 3), 3), ("vy", -1, 0), ("S", ("z", -1, 1, 4), 1),
    ("S", ("z", -1, 1, 3), 0), ("z", -1, 2, 0), ("xo", 1, 1, 3), ("S", ("z", 1, 1, 3), 2), ("xo", -1, -1, 1),
    ("vz", 1, 3), ("S", ("z", -1, 1, 4), 0), ("xo", -1, -1, 0), ("vz", -1, 3), ("S", ("z", -1, 1, 4), 3),
    ("S", ("z", 1, 1, 5), 0), ("z", 1, 2, 1), ("S", ("z", 1, 1, 5), 3), ("z", 1, 1, 2), ("S", ("z", 1, 1, 4), 2),
    ("z", 1, 3, 0), ("vy", 1, 2), ("S", ("z", -1, 1, 5), 1), ("vy", 1, -2), ("S", ("z", -1, 1, 5), 3), ("vy", 1, -1),
    ("S", ("z", 1, 1, 5), 2), ("S", ("z", 1, 1, 6), 0), ("xo", -1, -1, 2), ("S", ("z", -1, 1, 5), 0), ("z", -1, 1, 2),
    ("z", -1, 3, 1), ("z", 1, 1, 3), ("S", ("z", 1, 1, 4), 1), ("z", 1, 3, 1), ("vy", -1, 1), ("z", -1, 1, 3),
    ("z", -1, 2, 2), ("S", ("z", -1, 1, 4), 2), ("z", -1, 3, 0), ("vy", -1, -2), ("S", ("xo", 1, -1, 3)),
    ("vy", -1, 3), ("S", ("z", 1, 1, 5), 1), ("z", -1, 4, 1), ("z", 1, 2, 2), ("z", -1, 2, 3), ("z", 1, 1, 4),
    ("S", ("z", -1, 1, 6), 1), ("S", ("z", -1, 1, 6), 0), ("vyf", -1, 1), ("vyf", -1, 0), ("S", ("po", 1, -1, 1)),
    ("vy", 1, 3), ("vy", -1, 2), ("vyf", -1, -1), ("vy", 1, -3), ("z", -1, 3, 2), ("vyf", 1, 0),
    ("S", ("z", -1, 1, 6), 3), ("z", 1, 2, 3), ("vyf", -1, -2), ("S", ("z", -1, 1, 5), 2), ("vy", -1, -3),
    ("z", 1, 4, 0), ("z", 1, 1, 5), ("z", -1, 4, 0), ("G", "xo", 1), ("z", 1, 4, 1), ("S", ("po", 1, -1, 0)),
    ("z", -1, 3, 3), ("S", ("po", -1, 1, 1)), ("z", -1, 1, 4), ("vyf", -1, 3), ("S", ("z", 1, 1, 6), 1),
    ("S", ("z", -1, 1, 7), 1), ("S", ("z", 1, 1, 7), 1), ("G", "xf"), ("S", ("po", -1, 1, 0)), ("z", 1, 3, 2),
    ("S", ("z", 1, 1, 6), 3), ("vyf", 1, -2), ("S", ("z", -1, 1, 6), 2), ("G", "xo", -1), ("po", -1, -1, 0),
    ("z", -1, 4, 2), ("po", 1, 1, 0), ("vyf", -1, -3), ("S", ("z", -1, 1, 7), 3), ("vyf", 1, -1), ("vyf", 1, 1),
    ("S", ("po", 1, -1, 2)), ("po", -1, -1, 1), ("vyf", 1, 2), ("vyf", 1, -3), ("z", 1, 3, 3), ("z", 1, 2, 4),
    ("vyf", 1, 3), ("z", -1, 1, 5), ("S", ("z", 1, 1, 6), 2), ("vyf", -1, 2), ("z", 1, 4, 2), ("z", -1, 2, 4),
    ("G", "vk"), ("C", "oc", 2, 0), ("z", 1, 2, 5), ("z", -1, 4, 3), ("S", ("z", 1, 1, 7), 3),
    ("S", ("z", -1, 1, 7), 2), ("z", 1, 4, 3), ("S", ("z", 1, 1, 7), 0), ("S", ("po", -1, 1, 2)),
    ("S", ("z", -1, 1, 7), 0), ("S", ("po", -1, 1, 3)), ("G", "po", -1, 0), ("C", "oc", 2, 1), ("po", 1, 1, 1),
    ("S", ("po", 1, -1, 3)), ("z", -1, 2, 5), ("C", "oc", 0, 0), ("po", -1, -1, 2), ("z", 1, 3, 4),
    ("S", ("z", 1, 1, 7), 2), ("C", "oc", 1, 1), ("z", -1, 3, 4), ("G", "po", 1, 0), ("C", "oc", 0, 1),
    ("z", -1, 1, 6), ("po", 1, 1, 3), ("z", 1, 1, 6), ("po", 1, 1, 2), ("C", "oc", 1, 0), ("po", -1, -1, 3),
    ("z", -1, 1, 7), ("G", "pf", -1, 0), ("C", "oc", 6, 0), ("z", 1, 3, 5), ("C", "oc", 4, 0), ("z", -1, 3, 5),
    ("C", "oc", 3, 0), ("G", "po", -1, 1), ("z", 1, 4, 4), ("C", "oc", 3, 1), ("z", -1, 4, 4), ("z", 1, 1, 7),
    ("S", ("po", 1, -1, 4)), ("C", "oc", 7, 0), ("C", "oc", 5, 1), ("z", 1, 2, 6), ("S", ("po", -1, 1, 4)),
    ("z", -1, 2, 6), ("z", 1, 4, 5), ("S", ("po", -1, 1, 5)), ("C", "p3", 1, 0), ("C", "oc", 4, 1), ("G", "pf", 1, 0),
    ("z", 1, 2, 7), ("z", -1, 2, 7), ("z", -1, 4, 5), ("C", "oc", 5, 0), ("po", 1, 1, 4), ("C", "p3", 4, 1),
    ("G", "pf", 1, 1), ("z", 1, 3, 6), ("po", -1, -1, 4), ("z", -1, 3, 6), ("S", ("po", 1, -1, 5)),
    ("G", "po", -1, 2), ("G", "po", 1, 1), ("po", 1, 1, 5), ("z", -1, 3, 7), ("z", 1, 3, 7), ("po", -1, -1, 5),
    ("C", "p3", 4, 0), ("z", 1, 4, 6), ("z", -1, 4, 6), ("S", ("po", -1, 1, 6)), ("C", "p3", 2, 1),
    ("S", ("po", 1, -1, 6)), ("C", "oc", 7, 1), ("C", "p3", 2, 0), ("C", "p3", 0, 1), ("C", "p3", 1, 1),
    ("z", -1, 4, 7), ("z", 1, 4, 7), ("S", ("po", 1, -1, 7)), ("C", "oc", 6, 1), ("po", 1, 1, 6), ("G", "pf", -1, 2),
    ("G", "pf", -1, 1), ("S", ("po", -1, 1, 7)), ("C", "p3", 5, 1), ("C", "pl", 4, 0), ("G", "po", 1, 2),
    ("C", "p3", 6, 0), ("C", "pl", 1, 0), ("C", "p3", 0, 0), ("po", -1, -1, 6), ("G", "pf", 1, 2), ("C", "p3", 5, 0),
    ("po", 1, 1, 7), ("C", "pl", 2, 0), ("po", -1, -1, 7), ("C", "p3", 6, 1), ("G", "po", 1, 3), ("G", "po", -1, 3),
    ("C", "p3", 3, 0), ("C", "p3", 7, 0), ("C", "p3", 3, 1), ("C", "pl", 0, 0), ("C", "p3", 7, 1), ("C", "pl", 5, 0),
    ("C", "pl", 6, 0), ("G", "pf", 1, 3), ("G", "pf", -1, 3),
]


def starts():
    out = [(d, ("vz", d, 1)) for d in (1, -1)]
    out += [(None, ("z", d, 1, j)) for j in range(FIRST) for d in (1, -1)]
    out += [(None, ("vy", d, 0)) for d in (1, -1)]
    out.append((None, ("vk", 0, 0, 0)))
    return out


def follows(event):
    kind, out = event[0], []
    if kind == "xo":
        d, half, i = event[1:]
        if half == d:
            out.append((None, ("xf", d, d, i)))
    if kind == "z":
        d, h, j = event[1:]
        if h < HOPS:
            out.append((None, ("z", d, h + 1, j)))
        if h == HOPS:
            out.append((None, ("po", d, d, j)))
    if kind == "po":
        d, half, j = event[1:]
        if half == d:
            out.append((None, ("pf", d, d, j)))
    if kind == "vz":
        d, q = event[1:]
        if q < 3:
            out.append((d, ("vz", d, q + 1)))
        out += [(None, ("vy", 1, -d * q)), (None, ("vy", -1, -d * q))]
        out.append((None, ("vk", 0, 0, -d * q)))
    if kind == "vy":
        d, o = event[1:]
        out += [(None, ("vyf", d, o)), (None, ("vk", 1, d, o))]
    if kind == "vyf":
        d, o = event[1:]
        out.append((None, ("vk", 2, d, o)))
    return out


def offset(event):
    kind = event[0]
    if kind == "vz":
        return -event[1] * event[2]
    if kind in ("vy", "vyf"):
        return event[2]
    return event[3] if kind == "vk" else 0


def rows_of(half, pieces, i):
    return pl.ds((0 if half > 0 else 512) + sum(pieces[:i]), pieces[i])


def way(d):
    return 0 if d > 0 else 1


def group_of(event):
    kind = event[0]
    if kind == "xo" and event[1] != event[2]:
        return ("xo", event[1])
    if kind in ("xf", "vk"):
        return (kind,)
    if kind == "pf" or kind == "po" and event[1] != event[2]:
        return (kind, event[1], sum(ZROWS[: event[3]]) // TILE)
    return None


RECV = {
    "xo": (2, len(XROWS)),
    "z": (2, HOPS, len(ZROWS)),
    "po": (2, len(ZROWS)),
    "vz": (4,),
    "vy": (2, 4),
    "vyf": (2, 4),
    "Gxo": (2,),
    "Gxf": (1,),
    "Gvk": (1,),
    "Gpo": (2, 4),
    "Gpf": (2, 4),
}
SENT = {"x": (2,), "z": (2,), "y": (2,), "vk": (1,), "vz": (2, 3)}


def kernel(
    a_in, v_in, res_in, a_mask_in, v_mask_in, r_mask_in, out, a, v, keeps,
    res, relay, a_mask, v_mask, r_mask, load_sem, a_sem, *sems
):
    recv = dict(zip(RECV, sems[: len(RECV)]))
    sent = dict(zip(SENT, sems[len(RECV) :]))
    row, col = lax.axis_index("row"), lax.axis_index("col")
    zh, x = row // 4, row % 4
    zl, y, k = col // 8, (col // 2) % 4, col % 2
    z = 4 * zh + zl

    def at(dx=0, dy=0, dz=0, other=False):
        znew = (z + dz + 8) % 8
        return (
            4 * (znew // 4) + (x + dx + 4) % 4,
            8 * (znew % 4) + 2 * ((y + dy + 4) % 4) + (1 - k if other else k),
        )

    mine = lambda dx: 4 * zh + (x + dx + 4) % 4
    theirs = lambda dx: 4 * (1 - zh) + (x + dx + 4) % 4

    def v_rows(o, dy, half=0):
        start = (8 * (zl + o) + 2 * ((y + dy + 4) % 4) + k) * TILE
        if half == 0:
            return v.at[pl.ds(pl.multiple_of(start, TILE), TILE)]
        start = start + (0 if half > 0 else TILE // 2)
        return v.at[pl.ds(pl.multiple_of(start, TILE // 2), TILE // 2)]

    def copy(event, sending=True):
        kind = event[0]
        if kind in ("xo", "xf", "po", "pf"):
            d, half, i = event[1:]
            slot = (mine if kind[0] == "x" else theirs)(0 if kind[1] == "o" else -d)
            src = dst = a.at[slot, rows_of(half, XROWS if kind[0] == "x" else ZROWS, i)]
            to = at(dx=d)
        elif kind == "z":
            d, h, j = event[1:]
            rows = rows_of(d, ZROWS, j)
            src = a.at[mine(0), rows] if h == 1 else relay.at[max(h - 2, 0), rows]
            if h < HOPS:
                dst = relay.at[h - 1, rows]
            else:
                dst = a.at[4 * (1 - ((z + ZSTEP * d + 8) % 8) // 4) + x, rows]
            to = at(dz=ZSTEP * d)
        elif kind == "vz":
            d, q = event[1:]
            src = dst = v_rows(-d * (q - 1), 0)
            to = at(dz=d)
        elif kind == "vy":
            d, o = event[1:]
            src = dst = v_rows(o, 0)
            to = at(dy=d)
        elif kind == "vyf":
            d, o = event[1:]
            src = dst = v_rows(o, -d, d)
            to = at(dy=d)
        else:
            via, d, o = event[1:]
            src = dst = v_rows(o, -d * via, d if via == 2 else 0)
            to = at(other=True)
        arrived = recv_sem(event)
        if kind == "vz":
            arrived = arrived[0 if sending else 1]
        return remote(src, dst, sent_sem(event), arrived, to)

    def remote(src, dst, send_sem, recv_sem, to):
        return pltpu.make_async_remote_copy(
            src_ref=src, dst_ref=dst, send_sem=send_sem, recv_sem=recv_sem, device_id=to, device_id_type=MESH
        )

    def sent_sem(event):
        kind = event[0]
        if kind == "vk":
            return sent["vk"].at[0]
        if kind == "vz":
            return sent["vz"].at[way(event[1]), event[2] - 1]
        return sent["z" if kind == "z" else "y" if kind[0] == "v" else "x"].at[way(event[1])]

    def recv_sem(event):
        kind, group = event[0], group_of(event)
        if group is not None:
            return recv["G" + kind].at[tuple([way(group[1]), *group[2:]] if len(group) > 1 else [0])]
        if kind in ("xo", "po"):
            return recv[kind].at[way(event[1]), event[3]]
        if kind == "z":
            return recv[kind].at[way(event[1]), event[2] - 1, event[3]]
        if kind == "vz":
            return recv[kind].at[zl - event[1] * (event[2] - 1)], recv[kind].at[zl - event[1] * event[2]]
        return recv[kind].at[way(event[1]), zl + event[2]]

    def within(o, act):
        if o == 0:
            act()
        else:
            pl.when((zl + o >= 0) & (zl + o <= 3))(act)

    def start(step, event):
        go = lambda: copy(event).start()
        if step is None:
            go()
        else:
            within(step, go)

    def send_own(event, place=None):
        if place is None:
            start(None, event)
        else:
            here = zl if event[1] > 0 else 3 - zl
            pl.when(here == place)(lambda: start(None, event))

    def arrive(event):
        def act():
            copy(event, sending=False).wait_recv()
            for step, then in follows(event):
                start(step, then)

        within(offset(event), act)

    def arrive_group(kind, d=1, c=0):
        if kind == "xo":
            rows, slot = pl.ds(0 if d < 0 else 512, 512), mine(-d)
        elif kind == "xf":
            rows, slot = pl.ds(0, 1024), mine(2)
        elif kind == "po":
            rows, slot = pl.ds((0 if d < 0 else 512) + c * TILE, TILE), theirs(-d)
        elif kind == "pf":
            rows, slot = pl.ds((0 if d > 0 else 512) + c * TILE, TILE), theirs(2)
        held = v.at[pl.ds(0, 2048)] if kind == "vk" else a.at[slot, rows]
        sem = recv["G" + kind].at[tuple([way(d), c][: len(RECV["G" + kind])])]
        remote(held, held, sent["vk"].at[0], sem, at(other=True)).wait_recv()

    def departures():
        for d in (1, -1):
            for kind, held in (("x", a.at[pl.ds(0, 3)]), ("z", a.at[pl.ds(0, HOPS), pl.ds(0, 512)]), ("y", v.at[pl.ds(0, 768)])):
                remote(held, held, sent[kind].at[way(d)], recv["Gvk"].at[0], at(other=True)).wait_send()
            for q in (1, 2, 3):
                leave = lambda: copy(("vz", d, q)).wait_send()
                within(d, lambda: within(-d * (q - 1), leave))
        held = v.at[pl.ds(0, 2048)]
        remote(held, held, sent["vk"].at[0], recv["Gvk"].at[0], at(other=True)).wait_send()

    def product(slots, rows, cols):
        total = None
        for slot in slots:
            part = jnp.dot(
                a[slot, rows, :],
                v[pl.ds(pl.multiple_of(slot * 512, 512), 512), cols],
                preferred_element_type=jnp.float32,
            )
            total = part if total is None else total + part
        return total

    def multiply(which, c, n):
        rows = pl.ds(c * MROWS[which], MROWS[which])
        cols = pl.ds(n * NCOLS[which], NCOLS[which])
        slots = {
            "oc": [mine(dx) for dx in (0, 1, 2, 3)],
            "p3": [theirs(dx) for dx in (0, 1, 3)],
            "pl": [theirs(2)],
        }[which]
        total = product(slots, rows, cols)
        if which == "oc":
            out[rows, cols] = total
        elif which == "p3" and c not in LAST:
            out[rows, cols] += total
        else:
            total = total + out[rows, cols]
            for j in range(NCOLS[which] // TILE):
                at_tile = n * (NCOLS[which] // TILE) + j
                tile = pl.ds(at_tile * TILE, TILE)
                keep = r_mask[c, at_tile].astype(jnp.float32)
                out[rows, tile] = res[rows, tile].astype(jnp.float32) + keep * total[:, j * TILE : (j + 1) * TILE]
                if c in LAST:
                    keeps[LAST.index(c), :, tile] = jnp.full((8, TILE), keep)

    own_a = mine(0)
    own_v = pl.ds(pl.multiple_of(col * TILE, TILE), TILE)
    loads = {
        "am": pltpu.make_async_copy(a_mask_in, a_mask, load_sem.at[0]),
        "vm": pltpu.make_async_copy(v_mask_in, v_mask, load_sem.at[1]),
        "v": pltpu.make_async_copy(v_in, v.at[own_v], load_sem.at[2]),
        "res": pltpu.make_async_copy(res_in, res, load_sem.at[3]),
        "rm": pltpu.make_async_copy(r_mask_in, r_mask, load_sem.at[4]),
    }
    for half in (1, -1):
        for i in range(len(XROWS)):
            rows = rows_of(half, XROWS, i)
            loads[half, i] = pltpu.make_async_copy(
                a_in.at[rows], a.at[own_a, rows], a_sem.at[0 if half > 0 else 1, i]
            )
    for load in loads.values():
        load.start()

    barrier = pltpu.get_barrier_semaphore()
    neighbours = [at(dx=1), at(dx=-1), at(dy=1), at(dy=-1), at(dz=1), at(dz=-1), at(other=True)]
    if ZSTEP > 1:
        neighbours += [at(dz=ZSTEP), at(dz=-ZSTEP)]
    for neighbour in neighbours:
        pl.semaphore_signal(barrier, inc=1, device_id=neighbour, device_id_type=MESH)

    loads["am"].wait()
    loads["vm"].wait()

    def screen_a(half, i):
        loads[half, i].wait()
        first = (0 if half > 0 else 512) + sum(XROWS[:i])
        for t in range(first // TILE, (first + XROWS[i]) // TILE):
            rows = pl.ds(t * TILE, TILE)
            for j in range(4):
                cols = pl.ds(j * TILE, TILE)
                keep = a_mask[j, t].astype(jnp.float32)
                a[own_a, rows, cols] = (a[own_a, rows, cols].astype(jnp.float32) * keep).astype(jnp.bfloat16)

    def screen_v():
        loads["v"].wait()
        for j in range(8):
            cols = pl.ds(j * TILE, TILE)
            keep = v_mask[0, j].astype(jnp.float32)
            v[own_v, cols] = (v[own_v, cols].astype(jnp.float32) * keep).astype(jnp.bfloat16)

    for i in range(len(XROWS)):
        for half in (1, -1):
            screen_a(half, i)
            if i == 0 and half == 1:
                pl.semaphore_wait(barrier, len(neighbours))
            start(None, ("xo", half, half, i))
        if i == 0:
            screen_v()
            for step, event in starts():
                start(step, event)
    loads["res"].wait()
    loads["rm"].wait()
    for op in ORDER:
        if op[0] == "C":
            multiply(*op[1:])
        elif op[0] == "G":
            arrive_group(*op[1:])
        elif op[0] == "S":
            send_own(*op[1:])
        else:
            arrive(op)
    departures()


def finish(held, a, v, keeps, out, last, sem):
    spans = [pl.ds(0, 3 * TILE), pl.ds(4 * TILE, 3 * TILE)]
    copies = [pltpu.make_async_copy(held.at[rows], out.at[rows], sem.at[i]) for i, rows in enumerate(spans)]
    for copy in copies:
        copy.start()
    slot = 4 * (1 - lax.axis_index("row") // 4) + (lax.axis_index("row") + 2) % 4
    for i, c in enumerate(LAST):
        rows = pl.ds(c * TILE, TILE)
        block = v[pl.ds(pl.multiple_of(slot * 512, 512), 512), :]
        total = jnp.dot(a[slot, rows, :], block, preferred_element_type=jnp.float32)
        last[i] = held[rows, :] + keeps[i, 0:1, :] * total
        copies.append(pltpu.make_async_copy(last.at[i], out.at[rows], sem.at[2 + i]))
        copies[-1].start()
    for copy in copies:
        copy.wait()


def local(amplitudes, amplitude_mask, integrals, integral_mask, residual_in, residual_mask):
    hbm = pl.BlockSpec(memory_space=pltpu.HBM)
    vmem = pl.BlockSpec(memory_space=pltpu.VMEM)
    semaphores = [pltpu.SemaphoreType.DMA(shape) for shape in [*RECV.values(), *SENT.values()]]
    held = pl.pallas_call(
        kernel,
        out_shape=[
            pltpu.VMEM((1024, 1024), jnp.float32),
            pltpu.VMEM((8, 1024, 512), jnp.bfloat16),
            pltpu.VMEM((4096, 1024), jnp.bfloat16),
            pltpu.VMEM((len(LAST), 8, 1024), jnp.float32),
        ],
        in_specs=[hbm] * 6,
        out_specs=[vmem] * 4,
        scratch_shapes=[
            pltpu.VMEM((1024, 1024), jnp.bfloat16),
            pltpu.VMEM((max(HOPS - 1, 1), 1024, 512), jnp.bfloat16),
            pltpu.SMEM((4, 8), jnp.int32),
            pltpu.SMEM((1, 8), jnp.int32),
            pltpu.SMEM((8, 8), jnp.int32),
            pltpu.SemaphoreType.DMA((5,)),
            pltpu.SemaphoreType.DMA((2, len(XROWS))),
            *semaphores,
        ],
        compiler_params=pltpu.CompilerParams(
            collective_id=0, has_side_effects=True, vmem_limit_bytes=44 * 1024 * 1024 - 131072
        ),
        cost_estimate=pl.CostEstimate(flops=2 * 1024 * 4096 * 1024, bytes_accessed=12 << 20, transcendentals=0),
        name="ladder",
    )(amplitudes, integrals, residual_in, amplitude_mask.T, integral_mask, residual_mask)
    return pl.pallas_call(
        finish,
        out_shape=jax.ShapeDtypeStruct((1024, 1024), jnp.float32),
        in_specs=[vmem] * 4,
        out_specs=hbm,
        scratch_shapes=[pltpu.VMEM((len(LAST), TILE, 1024), jnp.float32), pltpu.SemaphoreType.DMA((2 + len(LAST),))],
        compiler_params=pltpu.CompilerParams(vmem_limit_bytes=16 * 1024 * 1024),
        name="finish",
    )(*held)


def solution(mesh):
    placed = P("col", "row")
    return jax.shard_map(
        local, mesh=mesh, in_specs=(placed,) * 6, out_specs=placed, check_vma=False
    )
```

```python
import functools

import jax
import jax.numpy as jnp
from jax import lax
from jax.experimental import pallas as pl
from jax.experimental.pallas import tpu as pltpu
from jax.sharding import PartitionSpec as P

MESH = pl.DeviceIdType.MESH
TILE = 128
XROWS = (128, 128, 128, 128)
ZROWS = (64, 64, 64, 64, 64, 64, 64, 64)
FIRST = 1
ZSTEP = 1
HOPS = 4 // ZSTEP

MROWS = {"oc": 128, "p3": 128, "pl": 128}
NCOLS = {"oc": 512, "p3": 512, "pl": 1024}
LAST = (3, 7)

ORDER = [
    ("S", ("z", 1, 1, 1), 0), ("S", ("xo", -1, 1, 2)), ("S", ("z", -1, 1, 1), 2), ("S", ("z", -1, 1, 1), 1),
    ("S", ("z", 1, 1, 1), 3), ("S", ("xo", 1, -1, 0)), ("S", ("z", 1, 1, 1), 2), ("S", ("z", 1, 1, 2), 0),
    ("vz", 1, 1), ("S", ("z", 1, 1, 1), 1), ("S", ("z", -1, 1, 1), 0), ("vz", -1, 1), ("z", 1, 1, 0), ("xo", 1, 1, 1),
    ("S", ("z", -1, 1, 2), 1), ("S", ("z", -1, 1, 3), 1), ("xo", 1, 1, 2), ("S", ("z", 1, 1, 2), 3),
    ("S", ("xo", 1, -1, 2)), ("S", ("z", 1, 1, 3), 0), ("S", ("z", 1, 1, 2), 1), ("S", ("xo", -1, 1, 3)),
    ("z", -1, 1, 1), ("S", ("xo", 1, -1, 1)), ("S", ("xo", -1, 1, 0)), ("S", ("z", -1, 1, 1), 3), ("z", -1, 1, 0),
    ("vz", 1, 2), ("S", ("z", 1, 1, 4), 0), ("z", 1, 2, 0), ("vz", -1, 2), ("xo", -1, -1, 3),
    ("S", ("z", 1, 1, 3), 3), ("z", -1, 2, 1), ("vy", -1, -1), ("S", ("z", 1, 1, 4), 3), ("vy", 1, 0),
    ("xo", 1, 1, 0), ("S", ("z", -1, 1, 2), 2), ("z", 1, 1, 1), ("S", ("z", 1, 1, 2), 2), ("S", ("z", -1, 1, 3), 2),
    ("S", ("z", -1, 1, 2), 0), ("S", ("z", -1, 1, 2), 3), ("vy", 1, 1), ("S", ("z", 1, 1, 3), 1),
    ("S", ("xo", -1, 1, 1)), ("S", ("z", -1, 1, 3), 3), ("vy", -1, 0), ("S", ("z", -1, 1, 4), 1),
    ("S", ("z", -1, 1, 3), 0), ("z", -1, 2, 0), ("xo", 1, 1, 3), ("S", ("z", 1, 1, 3), 2), ("xo", -1, -1, 1),
    ("vz", 1, 3), ("S", ("z", -1, 1, 4), 0), ("xo", -1, -1, 0), ("vz", -1, 3), ("S", ("z", -1, 1, 4), 3),
    ("S", ("z", 1, 1, 5), 0), ("z", 1, 2, 1), ("S", ("z", 1, 1, 5), 3), ("z", 1, 1, 2), ("S", ("z", 1, 1, 4), 2),
    ("z", 1, 3, 0), ("vy", 1, 2), ("S", ("z", -1, 1, 5), 1), ("vy", 1, -2), ("S", ("z", -1, 1, 5), 3), ("vy", 1, -1),
    ("S", ("z", 1, 1, 5), 2), ("S", ("z", 1, 1, 6), 0), ("xo", -1, -1, 2), ("S", ("z", -1, 1, 5), 0), ("z", -1, 1, 2),
    ("z", -1, 3, 1), ("z", 1, 1, 3), ("S", ("z", 1, 1, 4), 1), ("z", 1, 3, 1), ("vy", -1, 1), ("z", -1, 1, 3),
    ("z", -1, 2, 2), ("S", ("z", -1, 1, 4), 2), ("z", -1, 3, 0), ("vy", -1, -2), ("S", ("xo", 1, -1, 3)),
    ("vy", -1, 3), ("S", ("z", 1, 1, 5), 1), ("z", -1, 4, 1), ("z", 1, 2, 2), ("z", -1, 2, 3), ("z", 1, 1, 4),
    ("S", ("z", -1, 1, 6), 1), ("S", ("z", -1, 1, 6), 0), ("vyf", -1, 1), ("vyf", -1, 0), ("S", ("po", 1, -1, 1)),
    ("vy", 1, 3), ("vy", -1, 2), ("vyf", -1, -1), ("vy", 1, -3), ("z", -1, 3, 2), ("vyf", 1, 0),
    ("S", ("z", -1, 1, 6), 3), ("z", 1, 2, 3), ("vyf", -1, -2), ("S", ("z", -1, 1, 5), 2), ("vy", -1, -3),
    ("z", 1, 4, 0), ("z", 1, 1, 5), ("z", -1, 4, 0), ("G", "xo", 1), ("z", 1, 4, 1), ("S", ("po", 1, -1, 0)),
    ("z", -1, 3, 3), ("S", ("po", -1, 1, 1)), ("z", -1, 1, 4), ("vyf", -1, 3), ("S", ("z", 1, 1, 6), 1),
    ("S", ("z", -1, 1, 7), 1), ("S", ("z", 1, 1, 7), 1), ("G", "xf"), ("S", ("po", -1, 1, 0)), ("z", 1, 3, 2),
    ("S", ("z", 1, 1, 6), 3), ("vyf", 1, -2), ("S", ("z", -1, 1, 6), 2), ("G", "xo", -1), ("po", -1, -1, 0),
    ("z", -1, 4, 2), ("po", 1, 1, 0), ("vyf", -1, -3), ("S", ("z", -1, 1, 7), 3), ("vyf", 1, -1), ("vyf", 1, 1),
    ("S", ("po", 1, -1, 2)), ("po", -1, -1, 1), ("vyf", 1, 2), ("vyf", 1, -3), ("z", 1, 3, 3), ("z", 1, 2, 4),
    ("vyf", 1, 3), ("z", -1, 1, 5), ("S", ("z", 1, 1, 6), 2), ("vyf", -1, 2), ("z", 1, 4, 2), ("z", -1, 2, 4),
    ("G", "vk"), ("C", "oc", 2, 0), ("z", 1, 2, 5), ("z", -1, 4, 3), ("S", ("z", 1, 1, 7), 3),
    ("S", ("z", -1, 1, 7), 2), ("z", 1, 4, 3), ("S", ("z", 1, 1, 7), 0), ("S", ("po", -1, 1, 2)),
    ("S", ("z", -1, 1, 7), 0), ("S", ("po", -1, 1, 3)), ("G", "po", -1, 0), ("C", "oc", 2, 1), ("po", 1, 1, 1),
    ("S", ("po", 1, -1, 3)), ("z", -1, 2, 5), ("C", "oc", 0, 0), ("po", -1, -1, 2), ("z", 1, 3, 4),
    ("S", ("z", 1, 1, 7), 2), ("C", "oc", 1, 1), ("z", -1, 3, 4), ("G", "po", 1, 0), ("C", "oc", 0, 1),
    ("z", -1, 1, 6), ("po", 1, 1, 3), ("z", 1, 1, 6), ("po", 1, 1, 2), ("C", "oc", 1, 0), ("po", -1, -1, 3),
    ("z", -1, 1, 7), ("G", "pf", -1, 0), ("C", "oc", 6, 0), ("z", 1, 3, 5), ("C", "oc", 4, 0), ("z", -1, 3, 5),
    ("C", "oc", 3, 0), ("G", "po", -1, 1), ("z", 1, 4, 4), ("C", "oc", 3, 1), ("z", -1, 4, 4), ("z", 1, 1, 7),
    ("S", ("po", 1, -1, 4)), ("C", "oc", 7, 0), ("C", "oc", 5, 1), ("z", 1, 2, 6), ("S", ("po", -1, 1, 4)),
    ("z", -1, 2, 6), ("z", 1, 4, 5), ("S", ("po", -1, 1, 5)), ("C", "p3", 1, 0), ("C", "oc", 4, 1), ("G", "pf", 1, 0),
    ("z", 1, 2, 7), ("z", -1, 2, 7), ("z", -1, 4, 5), ("C", "oc", 5, 0), ("po", 1, 1, 4), ("C", "p3", 4, 1),
    ("G", "pf", 1, 1), ("z", 1, 3, 6), ("po", -1, -1, 4), ("z", -1, 3, 6), ("S", ("po", 1, -1, 5)),
    ("G", "po", -1, 2), ("G", "po", 1, 1), ("po", 1, 1, 5), ("z", -1, 3, 7), ("z", 1, 3, 7), ("po", -1, -1, 5),
    ("C", "p3", 4, 0), ("z", 1, 4, 6), ("z", -1, 4, 6), ("S", ("po", -1, 1, 6)), ("C", "p3", 2, 1),
    ("S", ("po", 1, -1, 6)), ("C", "oc", 7, 1), ("C", "p3", 2, 0), ("C", "p3", 0, 1), ("C", "p3", 1, 1),
    ("z", -1, 4, 7), ("z", 1, 4, 7), ("S", ("po", 1, -1, 7)), ("C", "oc", 6, 1), ("po", 1, 1, 6), ("G", "pf", -1, 2),
    ("G", "pf", -1, 1), ("S", ("po", -1, 1, 7)), ("C", "p3", 5, 1), ("C", "pl", 4, 0), ("G", "po", 1, 2),
    ("C", "p3", 6, 0), ("C", "pl", 1, 0), ("C", "p3", 0, 0), ("po", -1, -1, 6), ("G", "pf", 1, 2), ("C", "p3", 5, 0),
    ("po", 1, 1, 7), ("C", "pl", 2, 0), ("po", -1, -1, 7), ("C", "p3", 6, 1), ("G", "po", 1, 3), ("G", "po", -1, 3),
    ("C", "p3", 3, 0), ("C", "p3", 7, 0), ("C", "p3", 3, 1), ("C", "pl", 0, 0), ("C", "p3", 7, 1), ("C", "pl", 5, 0),
    ("C", "pl", 6, 0), ("G", "pf", 1, 3), ("G", "pf", -1, 3),
]


def starts():
    out = [(d, ("vz", d, 1)) for d in (1, -1)]
    out += [(None, ("z", d, 1, j)) for j in range(FIRST) for d in (1, -1)]
    out += [(None, ("vy", d, 0)) for d in (1, -1)]
    out.append((None, ("vk", 0, 0, 0)))
    return out


def follows(event):
    kind, out = event[0], []
    if kind == "xo":
        d, half, i = event[1:]
        if half == d:
            out.append((None, ("xf", d, d, i)))
    if kind == "z":
        d, h, j = event[1:]
        if h < HOPS:
            out.append((None, ("z", d, h + 1, j)))
        if h == HOPS:
            out.append((None, ("po", d, d, j)))
    if kind == "po":
        d, half, j = event[1:]
        if half == d:
            out.append((None, ("pf", d, d, j)))
    if kind == "vz":
        d, q = event[1:]
        if q < 3:
            out.append((d, ("vz", d, q + 1)))
        out += [(None, ("vy", 1, -d * q)), (None, ("vy", -1, -d * q))]
        out.append((None, ("vk", 0, 0, -d * q)))
    if kind == "vy":
        d, o = event[1:]
        out += [(None, ("vyf", d, o)), (None, ("vk", 1, d, o))]
    if kind == "vyf":
        d, o = event[1:]
        out.append((None, ("vk", 2, d, o)))
    return out


def offset(event):
    kind = event[0]
    if kind == "vz":
        return -event[1] * event[2]
    if kind in ("vy", "vyf"):
        return event[2]
    return event[3] if kind == "vk" else 0


def rows_of(half, pieces, i):
    return pl.ds((0 if half > 0 else 512) + sum(pieces[:i]), pieces[i])


def way(d):
    return 0 if d > 0 else 1


def group_of(event):
    kind = event[0]
    if kind == "xo" and event[1] != event[2]:
        return ("xo", event[1])
    if kind in ("xf", "vk"):
        return (kind,)
    if kind == "pf" or kind == "po" and event[1] != event[2]:
        return (kind, event[1], sum(ZROWS[: event[3]]) // TILE)
    return None


RECV = {
    "xo": (2, len(XROWS)),
    "z": (2, HOPS, len(ZROWS)),
    "po": (2, len(ZROWS)),
    "vz": (4,),
    "vy": (2, 4),
    "vyf": (2, 4),
    "Gxo": (2,),
    "Gxf": (1,),
    "Gvk": (1,),
    "Gpo": (2, 4),
    "Gpf": (2, 4),
}
SENT = {"x": (2,), "z": (2,), "y": (2,), "vk": (1,), "vz": (2, 3)}


def kernel(
    a_in, v_in, res_in, a_mask_in, v_mask_in, r_mask_in, out, a, v, keeps,
    res, relay, a_mask, v_mask, r_mask, load_sem, a_sem, *sems
):
    recv = dict(zip(RECV, sems[: len(RECV)]))
    sent = dict(zip(SENT, sems[len(RECV) :]))
    row, col = lax.axis_index("row"), lax.axis_index("col")
    zh, x = row // 4, row % 4
    zl, y, k = col // 8, (col // 2) % 4, col % 2
    z = 4 * zh + zl

    def at(dx=0, dy=0, dz=0, other=False):
        znew = (z + dz + 8) % 8
        return (
            4 * (znew // 4) + (x + dx + 4) % 4,
            8 * (znew % 4) + 2 * ((y + dy + 4) % 4) + (1 - k if other else k),
        )

    mine = lambda dx: 4 * zh + (x + dx + 4) % 4
    theirs = lambda dx: 4 * (1 - zh) + (x + dx + 4) % 4

    def v_rows(o, dy, half=0):
        start = (8 * (zl + o) + 2 * ((y + dy + 4) % 4) + k) * TILE
        if half == 0:
            return v.at[pl.ds(pl.multiple_of(start, TILE), TILE)]
        start = start + (0 if half > 0 else TILE // 2)
        return v.at[pl.ds(pl.multiple_of(start, TILE // 2), TILE // 2)]

    def copy(event, sending=True):
        kind = event[0]
        if kind in ("xo", "xf", "po", "pf"):
            d, half, i = event[1:]
            slot = (mine if kind[0] == "x" else theirs)(0 if kind[1] == "o" else -d)
            src = dst = a.at[slot, rows_of(half, XROWS if kind[0] == "x" else ZROWS, i)]
            to = at(dx=d)
        elif kind == "z":
            d, h, j = event[1:]
            rows = rows_of(d, ZROWS, j)
            src = a.at[mine(0), rows] if h == 1 else relay.at[max(h - 2, 0), rows]
            if h < HOPS:
                dst = relay.at[h - 1, rows]
            else:
                dst = a.at[4 * (1 - ((z + ZSTEP * d + 8) % 8) // 4) + x, rows]
            to = at(dz=ZSTEP * d)
        elif kind == "vz":
            d, q = event[1:]
            src = dst = v_rows(-d * (q - 1), 0)
            to = at(dz=d)
        elif kind == "vy":
            d, o = event[1:]
            src = dst = v_rows(o, 0)
            to = at(dy=d)
        elif kind == "vyf":
            d, o = event[1:]
            src = dst = v_rows(o, -d, d)
            to = at(dy=d)
        else:
            via, d, o = event[1:]
            src = dst = v_rows(o, -d * via, d if via == 2 else 0)
            to = at(other=True)
        arrived = recv_sem(event)
        if kind == "vz":
            arrived = arrived[0 if sending else 1]
        return remote(src, dst, sent_sem(event), arrived, to)

    def remote(src, dst, send_sem, recv_sem, to):
        return pltpu.make_async_remote_copy(
            src_ref=src, dst_ref=dst, send_sem=send_sem, recv_sem=recv_sem, device_id=to, device_id_type=MESH
        )

    def sent_sem(event):
        kind = event[0]
        if kind == "vk":
            return sent["vk"].at[0]
        if kind == "vz":
            return sent["vz"].at[way(event[1]), event[2] - 1]
        return sent["z" if kind == "z" else "y" if kind[0] == "v" else "x"].at[way(event[1])]

    def recv_sem(event):
        kind, group = event[0], group_of(event)
        if group is not None:
            return recv["G" + kind].at[tuple([way(group[1]), *group[2:]] if len(group) > 1 else [0])]
        if kind in ("xo", "po"):
            return recv[kind].at[way(event[1]), event[3]]
        if kind == "z":
            return recv[kind].at[way(event[1]), event[2] - 1, event[3]]
        if kind == "vz":
            return recv[kind].at[zl - event[1] * (event[2] - 1)], recv[kind].at[zl - event[1] * event[2]]
        return recv[kind].at[way(event[1]), zl + event[2]]

    def within(o, act):
        if o == 0:
            act()
        else:
            pl.when((zl + o >= 0) & (zl + o <= 3))(act)

    def start(step, event):
        go = lambda: copy(event).start()
        if step is None:
            go()
        else:
            within(step, go)

    def send_own(event, place=None):
        if place is None:
            start(None, event)
        else:
            here = zl if event[1] > 0 else 3 - zl
            pl.when(here == place)(lambda: start(None, event))

    def arrive(event):
        def act():
            copy(event, sending=False).wait_recv()
            for step, then in follows(event):
                start(step, then)

        within(offset(event), act)

    def arrive_group(kind, d=1, c=0):
        if kind == "xo":
            rows, slot = pl.ds(0 if d < 0 else 512, 512), mine(-d)
        elif kind == "xf":
            rows, slot = pl.ds(0, 1024), mine(2)
        elif kind == "po":
            rows, slot = pl.ds((0 if d < 0 else 512) + c * TILE, TILE), theirs(-d)
        elif kind == "pf":
            rows, slot = pl.ds((0 if d > 0 else 512) + c * TILE, TILE), theirs(2)
        held = v.at[pl.ds(0, 2048)] if kind == "vk" else a.at[slot, rows]
        sem = recv["G" + kind].at[tuple([way(d), c][: len(RECV["G" + kind])])]
        remote(held, held, sent["vk"].at[0], sem, at(other=True)).wait_recv()

    def departures():
        for d in (1, -1):
            for kind, held in (("x", a.at[pl.ds(0, 3)]), ("z", a.at[pl.ds(0, HOPS), pl.ds(0, 512)]), ("y", v.at[pl.ds(0, 768)])):
                remote(held, held, sent[kind].at[way(d)], recv["Gvk"].at[0], at(other=True)).wait_send()
            for q in (1, 2, 3):
                leave = lambda: copy(("vz", d, q)).wait_send()
                within(d, lambda: within(-d * (q - 1), leave))
        held = v.at[pl.ds(0, 2048)]
        remote(held, held, sent["vk"].at[0], recv["Gvk"].at[0], at(other=True)).wait_send()

    def product(slots, rows, cols):
        total = None
        for slot in slots:
            part = jnp.dot(
                a[slot, rows, :],
                v[pl.ds(pl.multiple_of(slot * 512, 512), 512), cols],
                preferred_element_type=jnp.float32,
            )
            total = part if total is None else total + part
        return total

    def multiply(which, c, n):
        rows = pl.ds(c * MROWS[which], MROWS[which])
        cols = pl.ds(n * NCOLS[which], NCOLS[which])
        slots = {
            "oc": [mine(dx) for dx in (0, 1, 2, 3)],
            "p3": [theirs(dx) for dx in (0, 1, 3)],
            "pl": [theirs(2)],
        }[which]
        total = product(slots, rows, cols)
        if which == "oc":
            out[rows, cols] = total
        elif which == "p3" and c not in LAST:
            out[rows, cols] += total
        else:
            total = total + out[rows, cols]
            for j in range(NCOLS[which] // TILE):
                at_tile = n * (NCOLS[which] // TILE) + j
                tile = pl.ds(at_tile * TILE, TILE)
                keep = r_mask[c, at_tile].astype(jnp.float32)
                out[rows, tile] = res[rows, tile].astype(jnp.float32) + keep * total[:, j * TILE : (j + 1) * TILE]
                if c in LAST:
                    keeps[LAST.index(c), :, tile] = jnp.full((8, TILE), keep)

    own_a = mine(0)
    own_v = pl.ds(pl.multiple_of(col * TILE, TILE), TILE)
    loads = {
        "am": pltpu.make_async_copy(a_mask_in, a_mask, load_sem.at[0]),
        "vm": pltpu.make_async_copy(v_mask_in, v_mask, load_sem.at[1]),
        "v": pltpu.make_async_copy(v_in, v.at[own_v], load_sem.at[2]),
        "res": pltpu.make_async_copy(res_in, res, load_sem.at[3]),
        "rm": pltpu.make_async_copy(r_mask_in, r_mask, load_sem.at[4]),
    }
    for half in (1, -1):
        for i in range(len(XROWS)):
            rows = rows_of(half, XROWS, i)
            loads[half, i] = pltpu.make_async_copy(
                a_in.at[rows], a.at[own_a, rows], a_sem.at[0 if half > 0 else 1, i]
            )
    order = ["am", (1, 0), (-1, 0), "vm", "v"]
    order += [(half, i) for i in range(1, len(XROWS)) for half in (1, -1)] + ["rm", "res"]
    for name in order:
        loads[name].start()

    barrier = pltpu.get_barrier_semaphore()
    neighbours = [at(dx=1), at(dx=-1), at(dy=1), at(dy=-1), at(dz=1), at(dz=-1), at(other=True)]
    if ZSTEP > 1:
        neighbours += [at(dz=ZSTEP), at(dz=-ZSTEP)]
    for neighbour in neighbours:
        pl.semaphore_signal(barrier, inc=1, device_id=neighbour, device_id_type=MESH)

    loads["am"].wait()
    loads["vm"].wait()

    def screen_a(half, i):
        loads[half, i].wait()
        first = (0 if half > 0 else 512) + sum(XROWS[:i])
        for t in range(first // TILE, (first + XROWS[i]) // TILE):
            rows = pl.ds(t * TILE, TILE)
            for j in range(4):
                cols = pl.ds(j * TILE, TILE)
                keep = a_mask[j, t].astype(jnp.float32)
                a[own_a, rows, cols] = (a[own_a, rows, cols].astype(jnp.float32) * keep).astype(jnp.bfloat16)

    def screen_v():
        loads["v"].wait()
        for j in range(8):
            cols = pl.ds(j * TILE, TILE)
            keep = v_mask[0, j].astype(jnp.float32)
            v[own_v, cols] = (v[own_v, cols].astype(jnp.float32) * keep).astype(jnp.bfloat16)

    for i in range(len(XROWS)):
        for half in (1, -1):
            screen_a(half, i)
            if i == 0 and half == 1:
                pl.semaphore_wait(barrier, len(neighbours))
            start(None, ("xo", half, half, i))
        if i == 0:
            screen_v()
            for step, event in starts():
                start(step, event)
    first = ORDER.index(next(op for op in ORDER if op[0] == "C"))
    for i, op in enumerate(ORDER):
        if i == first:
            loads["res"].wait()
            loads["rm"].wait()
        if op[0] == "C":
            multiply(*op[1:])
        elif op[0] == "G":
            arrive_group(*op[1:])
        elif op[0] == "S":
            send_own(*op[1:])
        else:
            arrive(op)
    departures()


def finish(held, a, v, keeps, out, last, sem):
    spans = [pl.ds(0, 3 * TILE), pl.ds(4 * TILE, 3 * TILE)]
    copies = [pltpu.make_async_copy(held.at[rows], out.at[rows], sem.at[i]) for i, rows in enumerate(spans)]
    for copy in copies:
        copy.start()
    slot = 4 * (1 - lax.axis_index("row") // 4) + (lax.axis_index("row") + 2) % 4
    for i, c in enumerate(LAST):
        rows = pl.ds(c * TILE, TILE)
        block = v[pl.ds(pl.multiple_of(slot * 512, 512), 512), :]
        total = jnp.dot(a[slot, rows, :], block, preferred_element_type=jnp.float32)
        last[i] = held[rows, :] + keeps[i, 0:1, :] * total
        copies.append(pltpu.make_async_copy(last.at[i], out.at[rows], sem.at[2 + i]))
        copies[-1].start()
    for copy in copies:
        copy.wait()


def local(amplitudes, amplitude_mask, integrals, integral_mask, residual_in, residual_mask):
    hbm = pl.BlockSpec(memory_space=pltpu.HBM)
    vmem = pl.BlockSpec(memory_space=pltpu.VMEM)
    semaphores = [pltpu.SemaphoreType.DMA(shape) for shape in [*RECV.values(), *SENT.values()]]
    held = pl.pallas_call(
        kernel,
        out_shape=[
            pltpu.VMEM((1024, 1024), jnp.float32),
            pltpu.VMEM((8, 1024, 512), jnp.bfloat16),
            pltpu.VMEM((4096, 1024), jnp.bfloat16),
            pltpu.VMEM((len(LAST), 8, 1024), jnp.float32),
        ],
        in_specs=[hbm] * 6,
        out_specs=[vmem] * 4,
        scratch_shapes=[
            pltpu.VMEM((1024, 1024), jnp.bfloat16),
            pltpu.VMEM((max(HOPS - 1, 1), 1024, 512), jnp.bfloat16),
            pltpu.SMEM((4, 8), jnp.int32),
            pltpu.SMEM((1, 8), jnp.int32),
            pltpu.SMEM((8, 8), jnp.int32),
            pltpu.SemaphoreType.DMA((5,)),
            pltpu.SemaphoreType.DMA((2, len(XROWS))),
            *semaphores,
        ],
        compiler_params=pltpu.CompilerParams(
            collective_id=0, has_side_effects=True, vmem_limit_bytes=44 * 1024 * 1024 - 131072
        ),
        cost_estimate=pl.CostEstimate(flops=2 * 1024 * 4096 * 1024, bytes_accessed=12 << 20, transcendentals=0),
        name="ladder",
    )(amplitudes, integrals, residual_in, amplitude_mask.T, integral_mask, residual_mask)
    return pl.pallas_call(
        finish,
        out_shape=jax.ShapeDtypeStruct((1024, 1024), jnp.float32),
        in_specs=[vmem] * 4,
        out_specs=hbm,
        scratch_shapes=[pltpu.VMEM((len(LAST), TILE, 1024), jnp.float32), pltpu.SemaphoreType.DMA((2 + len(LAST),))],
        compiler_params=pltpu.CompilerParams(vmem_limit_bytes=16 * 1024 * 1024),
        name="finish",
    )(*held)


def solution(mesh):
    placed = P("col", "row")
    return jax.shard_map(
        local, mesh=mesh, in_specs=(placed,) * 6, out_specs=placed, check_vma=False
    )
```
